128 devices in a mesh: row: 8 (over z, core), col: 16 (over y, x).
Axes of the slice: x: 4, y: 4, z: 4, core: 2. Of those that a mesh axis runs over, the one named last changes fastest.
Arguments:
- stiffness_blocks: float32 [1024, 20, 4096], P(('row', 'col')), as said below
- block_columns: int32 [1024, 20], P(('row', 'col')), may hold values from 0 to 7, as said below
- block_counts: int32 [1024, 5], P(('row', 'col')), may hold values from 0 to 4, as said below
- tentative_tiles: float32 [1024, 4096], P(('row', 'col')), may hold values from -1.5 to 1.5
- aggregate_of: int32 [1024], replicated, may hold values from 0 to 255, as said below
Outputs:
- coarse_operator: float32 [256, 64, 1664], P(('row', 'col'))
The draws below stay inside these ranges and needn't reach their ends.
Inputs may be any that keep to these rules, and one draw needn't show every extreme that they name: `block_columns`: the slots of one row in one class name different blocks; slot 0 names the row's own block, I % 8. `block_counts`: class 0 has 1 or more live slots; a class whose step leaves the grid has none; every device holds a row with 4 live slots in each class whose step stays in the grid. `aggregate_of`: the fine blocks of device d go to aggregates d * 2 to (d + 1) * 2 - 1, exactly 4 to each. `stiffness_blocks`: the diagonal entries of every row's slot 0 block lie between 2 and 10.
All inputs are finite; a program needn't handle non-finite values.
Results may differ from the reference program's by a relative error of at most 0.0003.
Values sent between devices are 32-bit elements; how exact they have to be, the bound alone decides.
A program may use at most 128 MiB of HBM per device.

```python
import math
import jax
import jax.numpy as jnp
import numpy as np
from jax import lax

FINE_DOF = 64
COARSE_DOF = 64
ROW_SLOTS = 4
NEIGHBORS = 5
OFFSETS = 13
BLOCKS_DEV = 8
SLOTS = 20
AGG_DEV = 2
AGGS_NEAR = 10
GRID_ROWS = 8
GRID_COLS = 16
FINE_BLOCKS = 1024
COARSE_BLOCKS = 256


def draw_stiffness_blocks(key, part):
    key = jax.random.fold_in(key, 11)
    noise_key, level_key = jax.random.split(key)
    full_shape = (FINE_BLOCKS, SLOTS, FINE_DOF * FINE_DOF)
    noise_part = jnp.clip(0.125 * jax.random.normal(noise_key, full_shape, jnp.float32), -0.5, 0.5)
    diag_level = jnp.exp(jax.random.uniform(level_key, (FINE_BLOCKS, FINE_DOF), jnp.float32, math.log(3.0), math.log(9.0)))
    identity_flat = (jnp.arange(FINE_DOF)[:, None] == jnp.arange(FINE_DOF)[None, :]).astype(jnp.float32)
    diag_boost = (diag_level[:, :, None] * identity_flat[None]).reshape(FINE_BLOCKS, FINE_DOF * FINE_DOF)
    slot_hit = (jnp.arange(SLOTS) == 0).astype(jnp.float32)
    return (noise_part + slot_hit[None, :, None] * diag_boost[:, None, :]).astype(jnp.float32)


def draw_block_columns(key, part):
    key = jax.random.fold_in(key, 21)
    row_ids = jnp.arange(FINE_BLOCKS, dtype=jnp.int32)
    own_local = row_ids % BLOCKS_DEV
    candidates = jnp.arange(BLOCKS_DEV, dtype=jnp.int32)
    scores = jax.random.randint(key, (FINE_BLOCKS, NEIGHBORS, BLOCKS_DEV), 0, 1 << 20, dtype=jnp.int32) * BLOCKS_DEV + candidates[None, None, :]
    own_hit = (jnp.arange(NEIGHBORS, dtype=jnp.int32)[None, :, None] == 0) & (candidates[None, None, :] == own_local[:, None, None])
    scores = jnp.where(own_hit, -1, scores)
    ordered = jnp.argsort(scores, axis=2, stable=True)[:, :, :ROW_SLOTS]
    return ordered.reshape(FINE_BLOCKS, SLOTS).astype(jnp.int32)


def draw_block_counts(key, part):
    key = jax.random.fold_in(key, 31)
    count_key, forced_key, level_key = jax.random.split(key, 3)
    row_ids = jnp.arange(FINE_BLOCKS, dtype=jnp.int32)
    device = row_ids // BLOCKS_DEV
    grid_row = device // GRID_COLS
    grid_col = device % GRID_COLS
    exists = jnp.stack([grid_row >= 0, grid_col > 0, grid_col < GRID_COLS - 1, grid_row > 0, grid_row < GRID_ROWS - 1], axis=1)
    device_cap = jax.random.randint(level_key, (FINE_BLOCKS // BLOCKS_DEV,), 1, ROW_SLOTS + 1, dtype=jnp.int32)
    raw_count = jax.random.randint(count_key, (FINE_BLOCKS, NEIGHBORS), 0, ROW_SLOTS + 1, dtype=jnp.int32)
    raw_count = jnp.minimum(raw_count, device_cap[device][:, None])
    own_class = jnp.arange(NEIGHBORS, dtype=jnp.int32)[None, :] == 0
    raw_count = jnp.where(own_class, jnp.maximum(raw_count, 1), raw_count)
    forced_row = jax.random.randint(forced_key, (FINE_BLOCKS // BLOCKS_DEV,), 0, BLOCKS_DEV, dtype=jnp.int32)
    row_hit = row_ids % BLOCKS_DEV == forced_row[device]
    counted = jnp.where(row_hit[:, None], ROW_SLOTS, raw_count)
    return jnp.where(exists, counted, 0).astype(jnp.int32)


def draw_aggregate_of(key, part):
    key = jax.random.fold_in(key, 41)
    device_count = FINE_BLOCKS // BLOCKS_DEV
    device_keys = jax.random.split(key, device_count)
    shuffles = jax.vmap(lambda each_key: jax.random.permutation(each_key, BLOCKS_DEV))(device_keys)
    owners = jnp.arange(device_count, dtype=jnp.int32)[:, None] * AGG_DEV
    return (owners + shuffles % AGG_DEV).reshape(FINE_BLOCKS).astype(jnp.int32)


def steps_of(own_key, dims, shards, smallest, largest):
    level, own = 1.0, jax.random.fold_in(own_key, 6)
    for axis_at, parts in shards:
        draws = jnp.exp(jax.random.uniform(jax.random.fold_in(own, axis_at), (parts,), jnp.float32, smallest / len(shards), largest / len(shards)))
        level = level * jnp.repeat(draws, dims[axis_at] // parts).reshape([-1 if axis == axis_at else 1 for axis in range(len(dims))])
    return level


def centred(stream_key, dims, spread, bound, cuts=(), kind=jnp.bfloat16):
    values = jax.random.normal(stream_key, dims, jnp.float32) * spread
    if len(cuts) > 0:
        values = steps_of(stream_key, dims, cuts, -0.22, 0.18) * values
    return jnp.clip(values, min=-bound, max=bound).astype(kind)


def setup_inputs(seed: int = 0) -> dict:
    key_list = jax.random.split(jax.random.key(seed), 6)
    stiffness_blocks = draw_stiffness_blocks(jax.random.fold_in(key_list[5], 71), 0)
    block_columns = draw_block_columns(jax.random.fold_in(key_list[5], 71), 0)
    block_counts = draw_block_counts(jax.random.fold_in(key_list[5], 71), 0)
    tentative_tiles = centred(key_list[3], (FINE_BLOCKS, FINE_DOF * COARSE_DOF), 0.25, 1.5, ((0, 128),), jnp.float32)
    aggregate_of = draw_aggregate_of(jax.random.fold_in(key_list[5], 71), 0)
    return {"stiffness_blocks": stiffness_blocks, "block_columns": block_columns, "block_counts": block_counts, "tentative_tiles": tentative_tiles, "aggregate_of": aggregate_of}


OMEGA = 2.0 / 3.0
CLASS_STEPS = ((0, 0), (0, -1), (0, 1), (-1, 0), (1, 0))
BAND_STEPS = ((-2, 0), (-1, -1), (-1, 0), (-1, 1), (0, -2), (0, -1), (0, 0), (0, 1), (0, 2), (1, -1), (1, 0), (1, 1), (2, 0))


def placement_table():
    placing = np.zeros((5, 5, 13), np.float32)
    for source in range(5):
        for target in range(5):
            offset = (CLASS_STEPS[target][0] - CLASS_STEPS[source][0], CLASS_STEPS[target][1] - CLASS_STEPS[source][1])
            placing[source, target, BAND_STEPS.index(offset)] = 1.0
    return placing


def reference(stiffness_blocks, block_columns, block_counts, tentative_tiles, aggregate_of):
    highest = lax.Precision.HIGHEST
    placing = jnp.asarray(placement_table(), dtype=jnp.float32)
    row_steps = jnp.array([class_step[0] for class_step in CLASS_STEPS], dtype=jnp.int32)
    col_steps = jnp.array([class_step[1] for class_step in CLASS_STEPS], dtype=jnp.int32)
    class_of = jnp.arange(SLOTS, dtype=jnp.int32) // ROW_SLOTS
    within = jnp.arange(SLOTS, dtype=jnp.int32) % ROW_SLOTS
    tile_rows = tentative_tiles.reshape(FINE_BLOCKS, FINE_DOF, COARSE_DOF)
    diagonal_slot = jnp.arange(SLOTS, dtype=jnp.int32) == 0
    tile_width = AGG_DEV * COARSE_DOF

    def one_device(running, device):
        grid_row = device // GRID_COLS
        grid_col = device % GRID_COLS
        near_device = jnp.clip(grid_row + row_steps, 0, GRID_ROWS - 1) * GRID_COLS + jnp.clip(grid_col + col_steps, 0, GRID_COLS - 1)
        first_row = (device * BLOCKS_DEV).astype(jnp.int32)
        stiff_rows = lax.dynamic_slice_in_dim(stiffness_blocks, first_row, BLOCKS_DEV, 0)
        column_rows = lax.dynamic_slice_in_dim(block_columns, first_row, BLOCKS_DEV, 0)
        count_rows = lax.dynamic_slice_in_dim(block_counts, first_row, BLOCKS_DEV, 0)
        own_tiles = lax.dynamic_slice_in_dim(tile_rows, first_row, BLOCKS_DEV, 0)
        live_mask = within[None, :] < jnp.take(count_rows, class_of, axis=1)
        blocks = jnp.where(live_mask[:, :, None], stiff_rows, 0.0).reshape(BLOCKS_DEV, SLOTS, FINE_DOF, FINE_DOF)
        fine_index = (near_device[class_of][None, :] * BLOCKS_DEV + column_rows).astype(jnp.int32)
        picked = jnp.take(tile_rows, fine_index, axis=0)
        stiff_tent = jnp.einsum("ksab,ksbc->ksac", blocks, picked, precision=highest)
        damping = OMEGA / jnp.diagonal(blocks[:, 0], axis1=1, axis2=2)
        smoothed = jnp.where(diagonal_slot[None, :, None, None], own_tiles[:, None], 0.0) - damping[:, None, :, None] * stiff_tent
        coarse_ids = jnp.take(aggregate_of, fine_index, axis=0)
        local_ids = class_of[None, :] * AGG_DEV + coarse_ids % AGG_DEV
        member = (local_ids[:, :, None] == jnp.arange(AGGS_NEAR, dtype=jnp.int32)[None, None, :]).astype(jnp.float32)
        left_side = jnp.einsum("ksg,ksfc->kfgc", member, smoothed, precision=highest).reshape(BLOCKS_DEV * FINE_DOF, AGGS_NEAR * COARSE_DOF)
        right_side = jnp.einsum("ksg,ksfc->kfgc", member, stiff_tent, precision=highest).reshape(BLOCKS_DEV * FINE_DOF, AGGS_NEAR * COARSE_DOF)
        pair_sums = lax.dot_general(left_side, right_side, (((0,), (0,)), ((), ())), precision=highest)
        pair_sums = pair_sums.reshape(NEIGHBORS, AGG_DEV, COARSE_DOF, NEIGHBORS, AGG_DEV, COARSE_DOF)
        banded = jnp.einsum("nxiyzj,nyo->nxiozj", pair_sums, placing, precision=highest)
        target = (near_device[:, None] * AGG_DEV + jnp.arange(AGG_DEV, dtype=jnp.int32)[None, :]).reshape(-1).astype(jnp.int32)
        running = running.at[target].add(banded.reshape(NEIGHBORS * AGG_DEV, COARSE_DOF, OFFSETS, AGG_DEV, COARSE_DOF))
        return running, None

    running = jnp.zeros((COARSE_BLOCKS, COARSE_DOF, OFFSETS, AGG_DEV, COARSE_DOF), jnp.float32)
    running, _ = lax.scan(one_device, running, jnp.arange(GRID_ROWS * GRID_COLS, dtype=jnp.int32))
    return running.reshape(COARSE_BLOCKS, COARSE_DOF, OFFSETS * tile_width)
```

```python
import jax
import jax.numpy as jnp
from jax import lax
from jax.experimental import pallas as pl
from jax.experimental.pallas import tpu as pltpu
from jax.sharding import PartitionSpec as P

MESH = pl.DeviceIdType.MESH
F32 = jnp.float32
BF16 = jnp.bfloat16

FINE = 64
BLOCKS = 8
SLOTS = 20
ROW_SLOTS = 4
CHUNKS = 32
LANES = 128
OMEGA = 2.0 / 3.0

STEPS = ((0, 0), (-1, 0), (1, 0), (0, -1), (0, 1))
CLASS = (0, 3, 4, 1, 2)
OPPOSITE = (0, 2, 1, 4, 3)
BAND_STEPS = (
    (-2, 0),
    (-1, -1),
    (-1, 0),
    (-1, 1),
    (0, -2),
    (0, -1),
    (0, 0),
    (0, 1),
    (0, 2),
    (1, -1),
    (1, 0),
    (1, 1),
    (2, 0),
)
OFFSETS = 13
NEAR = 5


def band_of(source, target):
    a, b = STEPS[source], STEPS[target]
    return BAND_STEPS.index((a[0] + b[0], a[1] + b[1]))


def dot(a, b):
    return jnp.dot(a, b, preferred_element_type=F32)


def split(x):
    high = x.astype(BF16)
    return high, (x - high.astype(F32)).astype(BF16)


def kernel(
    rows,
    cols,
    stiff,
    columns,
    counts,
    tiles,
    aggs,
    out,
    xbuf,
    compact,
    dense,
    tp,
    tpack,
    weights,
    damp,
    right,
    left,
    gsend,
    grecv,
    acc,
    xsem,
    tsem,
    osem,
    tsend,
    trecv,
    gsend_sem,
    grecv_sem,
):
    my_row = lax.axis_index("row")
    my_col = lax.axis_index("col")
    places = [
        (lax.rem(my_row + s[0] + rows, rows), lax.rem(my_col + s[1] + cols, cols)) for s in STEPS
    ]

    barrier = pltpu.get_barrier_semaphore()
    for q in range(1, NEAR):
        pl.semaphore_signal(barrier, inc=1, device_id=places[q], device_id_type=MESH)

    for i in range(CHUNKS):
        pltpu.make_async_copy(tiles.at[:, pl.ds(i * LANES, LANES)], tp.at[:, i, :], tsem).start()
    for i in range(CHUNKS):
        pltpu.make_async_copy(
            stiff.at[:, :, pl.ds(i * LANES, LANES)], xbuf.at[:, :, i, :], xsem
        ).start()

    lane = lax.broadcasted_iota(jnp.int32, (1, LANES), 1)
    low_half = lane < FINE
    half = jnp.where(low_half, 0, 1)

    pltpu.make_async_copy(tp, tp, tsem).wait()
    for pair in range(BLOCKS // 2):
        a, b = tp[2 * pair], tp[2 * pair + 1]
        tpack[0, pair, pl.ds(0, CHUNKS, 2), :] = jnp.where(low_half, a, pltpu.roll(b, FINE, 1))
        tpack[0, pair, pl.ds(1, CHUNKS, 2), :] = jnp.where(low_half, pltpu.roll(a, FINE, 1), b)

    pl.semaphore_wait(barrier, NEAR - 1)

    def tile_copy(q):
        return pltpu.make_async_remote_copy(
            src_ref=tpack.at[0],
            dst_ref=tpack.at[OPPOSITE[q]],
            send_sem=tsend.at[q],
            recv_sem=trecv.at[OPPOSITE[q]],
            device_id=places[q],
            device_id_type=MESH,
        )

    def arrival(q):
        return pltpu.make_async_remote_copy(
            src_ref=tpack.at[0],
            dst_ref=tpack.at[q],
            send_sem=tsend.at[q],
            recv_sem=trecv.at[q],
            device_id=places[q],
            device_id_type=MESH,
        )

    for q in (3, 4, 1, 2):
        tile_copy(q).start()

    weights[...] = jnp.zeros_like(weights)
    zero = jnp.zeros((CHUNKS, LANES), BF16)

    pltpu.make_async_copy(xbuf, xbuf, xsem).wait()

    row_at = lax.broadcasted_iota(jnp.int32, (CHUNKS, LANES), 0)
    lane_at = lax.broadcasted_iota(jnp.int32, (CHUNKS, LANES), 1)

    def spread(k, _):
        rows_k = pl.ds(pl.multiple_of(k * CHUNKS, CHUNKS), CHUNKS)
        x0 = xbuf[0, k]
        for p in range(2):
            diagonal = jnp.sum(
                jnp.where(lane_at == 2 * row_at + p * (FINE + 1), x0, 0.0), axis=1, keepdims=True
            )
            damp[p, rows_k, :] = jnp.broadcast_to(OMEGA / diagonal, (CHUNKS, LANES))
        for q in range(NEAR):
            compact[0, q, 0] = zero
            compact[1, q, 0] = zero
            count = counts[k, CLASS[q]]
            word = jnp.int32(0)
            for t in range(ROW_SLOTS):
                slot = CLASS[q] * ROW_SLOTS + t
                high, low = split(xbuf[slot, k])
                compact[0, q, t + 1] = high
                compact[1, q, t + 1] = low
                word = word | jnp.where(t < count, (t + 1) << (columns[k, slot] * 4), 0)
            for j in range(BLOCKS):
                e = (word >> (4 * j)) & 7
                lanes_j = slice(j * LANES, (j + 1) * LANES)
                dense[q, 0, rows_k, lanes_j] = compact[0, q, e]
                dense[q, 1, rows_k, lanes_j] = compact[1, q, e]
        return 0

    lax.fori_loop(0, BLOCKS, spread, 0)

    def near_aggs(q):
        first = (places[q][0] * cols + places[q][1]) * BLOCKS
        return [aggs[first + j] & 1 for j in range(BLOCKS)]

    def smooth(q):
        groups = near_aggs(q)
        for pair in range(BLOCKS // 2):
            v = tpack[q, pair]
            r = pltpu.roll(v, FINE, 1)
            both = (jnp.where(low_half, v, r), jnp.where(low_half, r, v))
            for side in range(2):
                j = 2 * pair + side
                high, low = split(jnp.where(half == groups[j], both[side], 0.0))
                for p in range(2):
                    rows_j = slice(j * LANES + p * FINE, j * LANES + (p + 1) * FINE)
                    weights[0, rows_j, p * LANES : (p + 1) * LANES] = high
                    weights[1, rows_j, p * LANES : (p + 1) * LANES] = low
        s = (
            dot(dense[q, 0], weights[0])
            + dot(dense[q, 1], weights[0])
            + dot(dense[q, 0], weights[1])
        )
        for p in range(2):
            s_p = s[:, p * LANES : (p + 1) * LANES]
            rows_p = slice(p * 256, (p + 1) * 256)
            high, low = split(s_p)
            right[0, rows_p, q * LANES : (q + 1) * LANES] = high
            right[1, rows_p, q * LANES : (q + 1) * LANES] = low
            l_p = -(damp[p] * s_p)
            if q == 0:
                own = []
                for k in range(BLOCKS):
                    t_k = tp[k]
                    r_k = pltpu.roll(t_k, FINE, 1)
                    t_both = jnp.where(low_half, t_k, r_k) if p == 0 else jnp.where(low_half, r_k, t_k)
                    own.append(jnp.where(half == groups[k], t_both, 0.0))
                l_p = l_p + jnp.concatenate(own, axis=0)
            high, low = split(l_p.T)
            left[0, q * LANES : (q + 1) * LANES, rows_p] = high
            left[1, q * LANES : (q + 1) * LANES, rows_p] = low

    def products(q_from, q_to, m_from, m_to):
        rows_l = slice(q_from * LANES, q_to * LANES)
        cols_r = slice(m_from * LANES, m_to * LANES)
        return (
            dot(left[0, rows_l, :], right[0, :, cols_r])
            + dot(left[1, rows_l, :], right[0, :, cols_r])
            + dot(left[0, rows_l, :], right[1, :, cols_r])
        )

    def piece_copy(q, m):
        return pltpu.make_async_remote_copy(
            src_ref=gsend.at[q, m],
            dst_ref=grecv.at[OPPOSITE[q], m],
            send_sem=gsend_sem.at[q, m],
            recv_sem=grecv_sem.at[OPPOSITE[q], m],
            device_id=places[q],
            device_id_type=MESH,
        )

    def piece_arrival(q, m):
        return pltpu.make_async_remote_copy(
            src_ref=gsend.at[q, m],
            dst_ref=grecv.at[q, m],
            send_sem=gsend_sem.at[q, m],
            recv_sem=grecv_sem.at[q, m],
            device_id=places[q],
            device_id_type=MESH,
        )

    def make_and_send(q_from, q_to, m_from, m_to):
        g = products(q_from, q_to, m_from, m_to)
        for m in range(m_from, m_to):
            for q in range(q_from, q_to):
                part = g[
                    (q - q_from) * LANES : (q - q_from + 1) * LANES,
                    (m - m_from) * LANES : (m - m_from + 1) * LANES,
                ]
                gsend[q, m] = part
                piece_copy(q, m).start()

    smooth(0)
    for q in (1, 2, 3, 4):
        arrival(q).wait_recv()
        smooth(q)
    for m_from, m_to in ((0, 2), (2, 4), (4, 5)):
        make_and_send(3, 5, m_from, m_to)
    for m_from, m_to in ((0, 2), (2, 4), (4, 5)):
        make_and_send(1, 3, m_from, m_to)
    own_products = products(0, 1, 0, NEAR)
    for m in range(NEAR):
        acc[band_of(0, m)] = own_products[:, m * LANES : (m + 1) * LANES]
    started = {band_of(0, m) for m in range(NEAR)}
    for m in range(NEAR):
        for q in (1, 2, 3, 4):
            piece_arrival(q, m).wait_recv()
            o = band_of(q, m)
            if o in started:
                acc[o] += grecv[q, m]
            else:
                acc[o] = grecv[q, m]
                started.add(o)

    def out_copy(o):
        return pltpu.make_async_copy(
            acc.at[o], out.at[:, pl.ds(o * LANES, LANES)], osem.at[o]
        )

    for o in range(OFFSETS):
        out_copy(o).start()
    for o in range(OFFSETS):
        out_copy(o).wait()
    for q in range(1, NEAR):
        tile_copy(q).wait_send()
        for m in range(NEAR):
            piece_copy(q, m).wait_send()


def solution(mesh):
    rows, cols = mesh.shape["row"], mesh.shape["col"]

    def body(stiffness_blocks, block_columns, block_counts, tentative_tiles, aggregate_of):
        any_spec = pl.BlockSpec(memory_space=pl.ANY)
        smem_spec = pl.BlockSpec(memory_space=pltpu.SMEM)
        dma = pltpu.SemaphoreType.DMA
        result = pl.pallas_call(
            lambda *refs: kernel(rows, cols, *refs),
            out_shape=jax.ShapeDtypeStruct((2 * FINE, OFFSETS * LANES), F32),
            in_specs=[any_spec, smem_spec, smem_spec, any_spec, smem_spec],
            out_specs=any_spec,
            scratch_shapes=[
                pltpu.VMEM((SLOTS, BLOCKS, CHUNKS, LANES), F32),
                pltpu.VMEM((2, NEAR, ROW_SLOTS + 1, CHUNKS, LANES), BF16),
                pltpu.VMEM((NEAR, 2, BLOCKS * CHUNKS, BLOCKS * LANES), BF16),
                pltpu.VMEM((BLOCKS, CHUNKS, LANES), F32),
                pltpu.VMEM((NEAR, BLOCKS // 2, FINE, LANES), F32),
                pltpu.VMEM((2, BLOCKS * LANES, 2 * LANES), BF16),
                pltpu.VMEM((2, BLOCKS * CHUNKS, LANES), F32),
                pltpu.VMEM((2, BLOCKS * FINE, NEAR * LANES), BF16),
                pltpu.VMEM((2, NEAR * LANES, BLOCKS * FINE), BF16),
                pltpu.VMEM((NEAR, NEAR, LANES, LANES), F32),
                pltpu.VMEM((NEAR, NEAR, LANES, LANES), F32),
                pltpu.VMEM((OFFSETS, LANES, LANES), F32),
                dma,
                dma,
                dma((OFFSETS,)),
                dma((NEAR,)),
                dma((NEAR,)),
                dma((NEAR, NEAR)),
                dma((NEAR, NEAR)),
            ],
            compiler_params=pltpu.CompilerParams(
                collective_id=0, has_side_effects=True, vmem_limit_bytes=56 << 20
            ),
        )(
            jnp.transpose(stiffness_blocks, (1, 0, 2)),
            block_columns,
            block_counts,
            tentative_tiles,
            aggregate_of,
        )
        return result.reshape(2, FINE, OFFSETS * LANES)

    by_device = P(("row", "col"), None)
    by_device3 = P(("row", "col"), None, None)
    return jax.shard_map(
        body,
        mesh=mesh,
        in_specs=(by_device3, by_device, by_device, by_device, P()),
        out_specs=by_device3,
        check_vma=False,
    )
```

```python
import jax
import jax.numpy as jnp
from jax import lax
from jax.experimental import pallas as pl
from jax.experimental.pallas import tpu as pltpu
from jax.sharding import PartitionSpec as P

MESH = pl.DeviceIdType.MESH
F32 = jnp.float32
BF16 = jnp.bfloat16

FINE = 64
BLOCKS = 8
SLOTS = 20
ROW_SLOTS = 4
CHUNKS = 32
LANES = 128
OMEGA = 2.0 / 3.0

STEPS = ((0, 0), (-1, 0), (1, 0), (0, -1), (0, 1))
CLASS = (0, 3, 4, 1, 2)
OPPOSITE = (0, 2, 1, 4, 3)
BAND_STEPS = (
    (-2, 0),
    (-1, -1),
    (-1, 0),
    (-1, 1),
    (0, -2),
    (0, -1),
    (0, 0),
    (0, 1),
    (0, 2),
    (1, -1),
    (1, 0),
    (1, 1),
    (2, 0),
)
OFFSETS = 13
NEAR = 5


def band_of(source, target):
    a, b = STEPS[source], STEPS[target]
    return BAND_STEPS.index((a[0] + b[0], a[1] + b[1]))


def dot(a, b):
    return jnp.dot(a, b, preferred_element_type=F32)


def split(x):
    high = x.astype(BF16)
    return high, (x - high.astype(F32)).astype(BF16)


def kernel(
    rows,
    cols,
    stiff,
    columns_in,
    counts_in,
    tiles,
    aggs_in,
    out,
    columns,
    counts,
    aggs,
    xbuf,
    compact,
    dense,
    tp,
    tpack,
    weights,
    damp,
    right,
    left,
    gsend,
    grecv,
    xsem,
    tsem,
    ssem,
    tsend,
    trecv,
    gsend_sem,
    grecv_sem,
):
    my_row = lax.axis_index("row")
    my_col = lax.axis_index("col")
    places = [(my_row + s[0], my_col + s[1]) for s in STEPS]
    exists = [
        None,
        my_row > 0,
        my_row < rows - 1,
        my_col > 0,
        my_col < cols - 1,
    ]

    barrier = pltpu.get_barrier_semaphore()
    near_count = jnp.int32(0)
    for q in range(1, NEAR):
        near_count = near_count + jnp.where(exists[q], 1, 0)

        @pl.when(exists[q])
        def _():
            pl.semaphore_signal(barrier, inc=1, device_id=places[q], device_id_type=MESH)

    for i in range(CHUNKS):
        pltpu.make_async_copy(tiles.at[:, pl.ds(i * LANES, LANES)], tp.at[:, i, :], tsem).start()
    small = [
        pltpu.make_async_copy(columns_in, columns, ssem.at[0]),
        pltpu.make_async_copy(counts_in, counts, ssem.at[1]),
        pltpu.make_async_copy(aggs_in, aggs, ssem.at[2]),
    ]
    for copy in small:
        copy.start()
    for i in range(CHUNKS):
        pltpu.make_async_copy(
            stiff.at[:, :, pl.ds(i * LANES, LANES)], xbuf.at[:, :, i, :], xsem
        ).start()

    lane = lax.broadcasted_iota(jnp.int32, (1, LANES), 1)
    low_half = lane < FINE
    half = jnp.where(low_half, 0, 1)

    pltpu.make_async_copy(tp, tp, tsem).wait()
    for pair in range(BLOCKS // 2):
        a, b = tp[2 * pair], tp[2 * pair + 1]
        tpack[0, pair, pl.ds(0, CHUNKS, 2), :] = jnp.where(low_half, a, pltpu.roll(b, FINE, 1))
        tpack[0, pair, pl.ds(1, CHUNKS, 2), :] = jnp.where(low_half, pltpu.roll(a, FINE, 1), b)

    pl.semaphore_wait(barrier, near_count)

    def tile_copy(q):
        return pltpu.make_async_remote_copy(
            src_ref=tpack.at[0],
            dst_ref=tpack.at[OPPOSITE[q]],
            send_sem=tsend.at[q],
            recv_sem=trecv.at[OPPOSITE[q]],
            device_id=places[q],
            device_id_type=MESH,
        )

    def arrival(q):
        return pltpu.make_async_remote_copy(
            src_ref=tpack.at[0],
            dst_ref=tpack.at[q],
            send_sem=tsend.at[q],
            recv_sem=trecv.at[q],
            device_id=places[q],
            device_id_type=MESH,
        )

    for q in (3, 4, 1, 2):

        @pl.when(exists[q])
        def _():
            tile_copy(q).start()

        @pl.when(jnp.logical_not(exists[q]))
        def _():
            tpack[q] = jnp.zeros((BLOCKS // 2, FINE, LANES), F32)

    own_bands = [band_of(0, m) for m in range(NEAR)]
    for o in range(OFFSETS):
        if o not in own_bands:
            out[:, o * LANES : (o + 1) * LANES] = jnp.zeros((LANES, LANES), F32)

    weights[...] = jnp.zeros_like(weights)
    zero = jnp.zeros((CHUNKS, LANES), BF16)

    for copy in small:
        copy.wait()
    pltpu.make_async_copy(xbuf, xbuf, xsem).wait()

    row_at = lax.broadcasted_iota(jnp.int32, (CHUNKS, LANES), 0)
    lane_at = lax.broadcasted_iota(jnp.int32, (CHUNKS, LANES), 1)

    def spread(k, _):
        rows_k = pl.ds(pl.multiple_of(k * CHUNKS, CHUNKS), CHUNKS)
        x0 = xbuf[0, k]
        for p in range(2):
            diagonal = jnp.sum(
                jnp.where(lane_at == 2 * row_at + p * (FINE + 1), x0, 0.0), axis=1, keepdims=True
            )
            damp[p, rows_k, :] = jnp.broadcast_to(OMEGA / diagonal, (CHUNKS, LANES))
        for q in range(NEAR):
            compact[0, q, 0] = zero
            compact[1, q, 0] = zero
            count = counts[k, CLASS[q]]
            word = jnp.int32(0)
            for t in range(ROW_SLOTS):
                slot = CLASS[q] * ROW_SLOTS + t
                high, low = split(xbuf[slot, k])
                compact[0, q, t + 1] = high
                compact[1, q, t + 1] = low
                word = word | jnp.where(t < count, (t + 1) << (columns[k, slot] * 4), 0)
            for j in range(BLOCKS):
                e = (word >> (4 * j)) & 7
                lanes_j = slice(j * LANES, (j + 1) * LANES)
                dense[q, 0, rows_k, lanes_j] = compact[0, q, e]
                dense[q, 1, rows_k, lanes_j] = compact[1, q, e]
        return 0

    lax.fori_loop(0, BLOCKS, spread, 0)

    def near_aggs(q):
        near_row = jnp.clip(places[q][0], 0, rows - 1)
        near_col = jnp.clip(places[q][1], 0, cols - 1)
        first = (near_row * cols + near_col) * BLOCKS
        return [aggs[first + j] & 1 for j in range(BLOCKS)]

    def smooth(q):
        groups = near_aggs(q)
        for pair in range(BLOCKS // 2):
            v = tpack[q, pair]
            r = pltpu.roll(v, FINE, 1)
            both = (jnp.where(low_half, v, r), jnp.where(low_half, r, v))
            for side in range(2):
                j = 2 * pair + side
                high, low = split(jnp.where(half == groups[j], both[side], 0.0))
                for p in range(2):
                    rows_j = slice(j * LANES + p * FINE, j * LANES + (p + 1) * FINE)
                    weights[0, rows_j, p * LANES : (p + 1) * LANES] = high
                    weights[1, rows_j, p * LANES : (p + 1) * LANES] = low
        s = (
            dot(dense[q, 0], weights[0])
            + dot(dense[q, 1], weights[0])
            + dot(dense[q, 0], weights[1])
        )
        for p in range(2):
            s_p = s[:, p * LANES : (p + 1) * LANES]
            rows_p = slice(p * 256, (p + 1) * 256)
            high, low = split(s_p)
            right[0, rows_p, q * LANES : (q + 1) * LANES] = high
            right[1, rows_p, q * LANES : (q + 1) * LANES] = low
            l_p = -(damp[p] * s_p)
            if q == 0:
                own = []
                for k in range(BLOCKS):
                    t_k = tp[k]
                    r_k = pltpu.roll(t_k, FINE, 1)
                    t_both = jnp.where(low_half, t_k, r_k) if p == 0 else jnp.where(low_half, r_k, t_k)
                    own.append(jnp.where(half == groups[k], t_both, 0.0))
                l_p = l_p + jnp.concatenate(own, axis=0)
            high, low = split(l_p.T)
            left[0, q * LANES : (q + 1) * LANES, rows_p] = high
            left[1, q * LANES : (q + 1) * LANES, rows_p] = low

    def products(q_from, q_to, m_from, m_to):
        rows_l = slice(q_from * LANES, q_to * LANES)
        cols_r = slice(m_from * LANES, m_to * LANES)
        return (
            dot(left[0, rows_l, :], right[0, :, cols_r])
            + dot(left[1, rows_l, :], right[0, :, cols_r])
            + dot(left[0, rows_l, :], right[1, :, cols_r])
        )

    def piece_copy(q, m):
        return pltpu.make_async_remote_copy(
            src_ref=gsend.at[q, m],
            dst_ref=grecv.at[OPPOSITE[q], m],
            send_sem=gsend_sem.at[q, m],
            recv_sem=grecv_sem.at[OPPOSITE[q], m],
            device_id=places[q],
            device_id_type=MESH,
        )

    def piece_arrival(q, m):
        return pltpu.make_async_remote_copy(
            src_ref=gsend.at[q, m],
            dst_ref=grecv.at[q, m],
            send_sem=gsend_sem.at[q, m],
            recv_sem=grecv_sem.at[q, m],
            device_id=places[q],
            device_id_type=MESH,
        )

    def make_and_send(q_from, q_to, m_from, m_to):
        g = products(q_from, q_to, m_from, m_to)
        for q in range(q_from, q_to):
            for m in range(m_from, m_to):
                part = g[
                    (q - q_from) * LANES : (q - q_from + 1) * LANES,
                    (m - m_from) * LANES : (m - m_from + 1) * LANES,
                ]
                if q == 0:
                    o = own_bands[m]
                    out[:, o * LANES : (o + 1) * LANES] = part
                else:
                    gsend[q, m] = part
        for q in range(max(q_from, 1), q_to):

            @pl.when(exists[q])
            def _():
                for m in range(m_from, m_to):
                    piece_copy(q, m).start()

    def wait_tiles(q):
        @pl.when(exists[q])
        def _():
            arrival(q).wait_recv()

    smooth(0)
    wait_tiles(1)
    smooth(1)
    wait_tiles(2)
    smooth(2)
    make_and_send(1, 3, 0, 2)
    make_and_send(1, 3, 2, 3)
    make_and_send(0, 1, 0, 3)
    wait_tiles(3)
    smooth(3)
    wait_tiles(4)
    smooth(4)
    make_and_send(3, 5, 0, 2)
    make_and_send(3, 5, 2, 4)
    make_and_send(3, 5, 4, 5)
    make_and_send(1, 3, 3, 5)
    make_and_send(0, 1, 3, 5)
    for q_group, m_group in (((1, 2), range(0, 3)), ((3, 4), range(0, 3)), ((1, 2), range(3, 5)), ((3, 4), range(3, 5))):
        for m in m_group:
            for q in q_group:

                @pl.when(exists[q])
                def _():
                    piece_arrival(q, m).wait_recv()
                    o = band_of(q, m)
                    out[:, o * LANES : (o + 1) * LANES] += grecv[q, m]

    for q in range(1, NEAR):

        @pl.when(exists[q])
        def _():
            tile_copy(q).wait_send()
            for m in range(NEAR):
                piece_copy(q, m).wait_send()


def solution(mesh):
    rows, cols = mesh.shape["row"], mesh.shape["col"]

    def body(stiffness_blocks, block_columns, block_counts, tentative_tiles, aggregate_of):
        any_spec = pl.BlockSpec(memory_space=pl.ANY)
        in_hbm = lambda x: pltpu.with_memory_space_constraint(x, pltpu.HBM)
        dma = pltpu.SemaphoreType.DMA
        result = pl.pallas_call(
            lambda *refs: kernel(rows, cols, *refs),
            out_shape=jax.ShapeDtypeStruct((2 * FINE, OFFSETS * LANES), F32),
            in_specs=[any_spec] * 5,
            out_specs=pl.BlockSpec(memory_space=pltpu.VMEM),
            scratch_shapes=[
                pltpu.SMEM((BLOCKS, SLOTS), jnp.int32),
                pltpu.SMEM((BLOCKS, NEAR), jnp.int32),
                pltpu.SMEM(aggregate_of.shape, jnp.int32),
                pltpu.VMEM((SLOTS, BLOCKS, CHUNKS, LANES), F32),
                pltpu.VMEM((2, NEAR, ROW_SLOTS + 1, CHUNKS, LANES), BF16),
                pltpu.VMEM((NEAR, 2, BLOCKS * CHUNKS, BLOCKS * LANES), BF16),
                pltpu.VMEM((BLOCKS, CHUNKS, LANES), F32),
                pltpu.VMEM((NEAR, BLOCKS // 2, FINE, LANES), F32),
                pltpu.VMEM((2, BLOCKS * LANES, 2 * LANES), BF16),
                pltpu.VMEM((2, BLOCKS * CHUNKS, LANES), F32),
                pltpu.VMEM((2, BLOCKS * FINE, NEAR * LANES), BF16),
                pltpu.VMEM((2, NEAR * LANES, BLOCKS * FINE), BF16),
                pltpu.VMEM((NEAR, NEAR, LANES, LANES), F32),
                pltpu.VMEM((NEAR, NEAR, LANES, LANES), F32),
                dma,
                dma,
                dma((3,)),
                dma((NEAR,)),
                dma((NEAR,)),
                dma((NEAR, NEAR)),
                dma((NEAR, NEAR)),
            ],
            compiler_params=pltpu.CompilerParams(
                collective_id=0, has_side_effects=True, vmem_limit_bytes=40 << 20
            ),
        )(
            in_hbm(jnp.transpose(stiffness_blocks, (1, 0, 2))),
            in_hbm(block_columns),
            in_hbm(block_counts),
            in_hbm(tentative_tiles),
            in_hbm(aggregate_of),
        )
        return result.reshape(2, FINE, OFFSETS * LANES)

    by_device = P(("row", "col"), None)
    by_device3 = P(("row", "col"), None, None)
    return jax.shard_map(
        body,
        mesh=mesh,
        in_specs=(by_device3, by_device, by_device, by_device, P()),
        out_specs=by_device3,
        check_vma=False,
    )
```

```python
import jax
import jax.numpy as jnp
from jax import lax
from jax.experimental import pallas as pl
from jax.experimental.pallas import tpu as pltpu
from jax.sharding import PartitionSpec as P

MESH = pl.DeviceIdType.MESH
F32 = jnp.float32
BF16 = jnp.bfloat16

FINE = 64
BLOCKS = 8
SLOTS = 20
ROW_SLOTS = 4
CHUNKS = 32
LANES = 128
OMEGA = 2.0 / 3.0

STEPS = ((0, 0), (-1, 0), (1, 0), (0, -1), (0, 1))
CLASS = (0, 3, 4, 1, 2)
OPPOSITE = (0, 2, 1, 4, 3)
BAND_STEPS = (
    (-2, 0),
    (-1, -1),
    (-1, 0),
    (-1, 1),
    (0, -2),
    (0, -1),
    (0, 0),
    (0, 1),
    (0, 2),
    (1, -1),
    (1, 0),
    (1, 1),
    (2, 0),
)
OFFSETS = 13
NEAR = 5


def band_of(source, target):
    a, b = STEPS[source], STEPS[target]
    return BAND_STEPS.index((a[0] + b[0], a[1] + b[1]))


def dot(a, b):
    return jnp.dot(a, b, preferred_element_type=F32)


def split(x):
    high = x.astype(BF16)
    return high, (x - high.astype(F32)).astype(BF16)


def kernel(
    rows,
    cols,
    stiff,
    columns_in,
    counts_in,
    tiles,
    aggs_in,
    out,
    columns,
    counts,
    aggs,
    xbuf,
    compact,
    dense,
    order,
    tp,
    tpack,
    weights,
    halves,
    damp,
    right,
    left,
    gsend,
    grecv,
    xsem,
    tsem,
    ssem,
    tsend,
    trecv,
    gsend_sem,
    grecv_sem,
):
    my_row = lax.axis_index("row")
    my_col = lax.axis_index("col")
    places = [(my_row + s[0], my_col + s[1]) for s in STEPS]
    exists = [
        None,
        my_row > 0,
        my_row < rows - 1,
        my_col > 0,
        my_col < cols - 1,
    ]

    barrier = pltpu.get_barrier_semaphore()
    near_count = jnp.int32(0)
    for q in range(1, NEAR):
        near_count = near_count + jnp.where(exists[q], 1, 0)

        @pl.when(exists[q])
        def _():
            pl.semaphore_signal(barrier, inc=1, device_id=places[q], device_id_type=MESH)

    for i in range(CHUNKS):
        pltpu.make_async_copy(tiles.at[:, pl.ds(i * LANES, LANES)], tp.at[:, i, :], tsem).start()
    small = [
        pltpu.make_async_copy(columns_in, columns, ssem.at[0]),
        pltpu.make_async_copy(counts_in, counts, ssem.at[1]),
        pltpu.make_async_copy(aggs_in, aggs, ssem.at[2]),
    ]
    for copy in small:
        copy.start()
    for first, last, sem in ((0, ROW_SLOTS, xsem.at[0]), (ROW_SLOTS, SLOTS, xsem.at[1])):
        for i in range(CHUNKS):
            pltpu.make_async_copy(
                stiff.at[first:last, :, pl.ds(i * LANES, LANES)], xbuf.at[first:last, :, i, :], sem
            ).start()

    lane = lax.broadcasted_iota(jnp.int32, (1, LANES), 1)
    low_half = lane < FINE
    half = jnp.where(low_half, 0, 1)

    for copy in small:
        copy.wait()
    own_groups = None
    for q in range(NEAR):
        near_row = jnp.clip(places[q][0], 0, rows - 1)
        near_col = jnp.clip(places[q][1], 0, cols - 1)
        first = (near_row * cols + near_col) * BLOCKS
        groups = [aggs[first + j] & 1 for j in range(BLOCKS)]
        word = jnp.int32(0)
        ones = jnp.int32(0)
        for j in range(BLOCKS):
            at = jnp.where(groups[j] == 1, 4 + ones, j - ones)
            word = word | (jnp.int32(j) << (4 * at))
            ones = ones + groups[j]
        if q == 0:
            own_groups = groups
        for n in range(BLOCKS):
            order[q, n] = (word >> (4 * n)) & 7

    pltpu.make_async_copy(tp, tp, tsem).wait()
    for group in range(2):
        for pair in range(2):
            a = tp[order[0, 4 * group + 2 * pair]]
            b = tp[order[0, 4 * group + 2 * pair + 1]]
            tpack[0, group, pair, pl.ds(0, CHUNKS, 2), :] = jnp.where(low_half, a, pltpu.roll(b, FINE, 1))
            tpack[0, group, pair, pl.ds(1, CHUNKS, 2), :] = jnp.where(low_half, pltpu.roll(a, FINE, 1), b)

    def tile_copy(q, group):
        return pltpu.make_async_remote_copy(
            src_ref=tpack.at[0, group],
            dst_ref=tpack.at[OPPOSITE[q], group],
            send_sem=tsend.at[q, group],
            recv_sem=trecv.at[OPPOSITE[q], group],
            device_id=places[q],
            device_id_type=MESH,
        )

    def arrival(q, group):
        return pltpu.make_async_remote_copy(
            src_ref=tpack.at[0, group],
            dst_ref=tpack.at[q, group],
            send_sem=tsend.at[q, group],
            recv_sem=trecv.at[q, group],
            device_id=places[q],
            device_id_type=MESH,
        )

    own_bands = [band_of(0, m) for m in range(NEAR)]

    row_at = lax.broadcasted_iota(jnp.int32, (CHUNKS, LANES), 0)
    lane_at = lax.broadcasted_iota(jnp.int32, (CHUNKS, LANES), 1)

    zero = jnp.zeros((CHUNKS, LANES), BF16)
    for q in range(NEAR):
        compact[q, 0, 0] = zero
        compact[q, 1, 0] = zero

    def spread(q, slots, k):
        rows_k = pl.ds(pl.multiple_of(k * CHUNKS, CHUNKS), CHUNKS)
        rows_low = pl.ds(pl.multiple_of(k * CHUNKS + 256, CHUNKS), CHUNKS)
        count = counts[k, slots // ROW_SLOTS]
        word = jnp.int32(0)
        for t in range(ROW_SLOTS):
            high, low = split(xbuf[slots + t, k])
            compact[q, 0, t + 1] = high
            compact[q, 1, t + 1] = low
            word = word | jnp.where(t < count, (t + 1) << (columns[k, slots + t] * 4), 0)
        for group in range(2):
            for n in range(4):
                e = (word >> (4 * order[q, 4 * group + n])) & 7
                lanes_n = slice(n * LANES, (n + 1) * LANES)
                dense[q, group, rows_k, lanes_n] = compact[q, 0, e]
                dense[q, group, rows_low, lanes_n] = compact[q, 1, e]

    def spread_own(k, _):
        rows_k = pl.ds(pl.multiple_of(k * CHUNKS, CHUNKS), CHUNKS)
        x0 = xbuf[0, k]
        for p in range(2):
            diagonal = jnp.sum(
                jnp.where(lane_at == 2 * row_at + p * (FINE + 1), x0, 0.0), axis=1, keepdims=True
            )
            damp[p, rows_k, :] = jnp.broadcast_to(OMEGA / diagonal, (CHUNKS, LANES))
        spread(0, 0, k)
        return 0

    def spread_near(k, _):
        for q in range(1, NEAR):
            spread(q, CLASS[q] * ROW_SLOTS, k)
        return 0

    def smooth_half(q, group):
        for pair in range(2):
            v = tpack[q, group, pair]
            r = pltpu.roll(v, FINE, 1)
            for part, (v_part, r_part) in enumerate(zip(split(v), split(r))):
                lanes_part = slice(part * LANES, (part + 1) * LANES)
                none = jnp.zeros_like(v_part)
                tiles_at = (
                    jnp.where(low_half, v_part, none),
                    jnp.where(low_half, none, r_part),
                    jnp.where(low_half, r_part, none),
                    jnp.where(low_half, none, v_part),
                )
                for n in range(4):
                    rows_n = slice((4 * pair + n) * FINE, (4 * pair + n + 1) * FINE)
                    weights[group, rows_n, lanes_part] = tiles_at[n]
        x = dot(dense[q, group], weights[group])
        halves[q, group] = x[:256, :LANES] + (x[:256, LANES:] + x[256:, :LANES])

    def finish(q):
        s_0, s_1 = halves[q, 0], halves[q, 1]
        by_parity = (
            jnp.where(low_half, s_0, pltpu.roll(s_1, FINE, 1)),
            jnp.where(low_half, pltpu.roll(s_0, FINE, 1), s_1),
        )
        for p in range(2):
            s_p = by_parity[p]
            rows_p = slice(p * 256, (p + 1) * 256)
            high, low = split(s_p)
            right[0, rows_p, q * LANES : (q + 1) * LANES] = high
            right[1, rows_p, q * LANES : (q + 1) * LANES] = low
            l_p = -(damp[p] * s_p)
            if q == 0:
                own = []
                for k in range(BLOCKS):
                    t_k = tp[k]
                    r_k = pltpu.roll(t_k, FINE, 1)
                    t_both = jnp.where(low_half, t_k, r_k) if p == 0 else jnp.where(low_half, r_k, t_k)
                    own.append(jnp.where(half == own_groups[k], t_both, 0.0))
                l_p = l_p + jnp.concatenate(own, axis=0)
            high, low = split(l_p.T)
            left[0, q * LANES : (q + 1) * LANES, rows_p] = high
            left[1, q * LANES : (q + 1) * LANES, rows_p] = low

    def products(q_from, q_to, m_from, m_to):
        rows_l = slice(q_from * LANES, q_to * LANES)
        cols_r = slice(m_from * LANES, m_to * LANES)
        return (
            dot(left[0, rows_l, :], right[0, :, cols_r])
            + dot(left[1, rows_l, :], right[0, :, cols_r])
            + dot(left[0, rows_l, :], right[1, :, cols_r])
        )

    def piece_copy(q, m):
        return pltpu.make_async_remote_copy(
            src_ref=gsend.at[q, m],
            dst_ref=grecv.at[OPPOSITE[q], m],
            send_sem=gsend_sem.at[q, m],
            recv_sem=grecv_sem.at[OPPOSITE[q], m],
            device_id=places[q],
            device_id_type=MESH,
        )

    def piece_arrival(q, m):
        return pltpu.make_async_remote_copy(
            src_ref=gsend.at[q, m],
            dst_ref=grecv.at[q, m],
            send_sem=gsend_sem.at[q, m],
            recv_sem=grecv_sem.at[q, m],
            device_id=places[q],
            device_id_type=MESH,
        )

    def make_and_send(q_from, q_to, m_from, m_to):
        g = products(q_from, q_to, m_from, m_to)
        for q in range(q_from, q_to):
            for m in range(m_from, m_to):
                part = g[
                    (q - q_from) * LANES : (q - q_from + 1) * LANES,
                    (m - m_from) * LANES : (m - m_from + 1) * LANES,
                ]
                if q == 0:
                    o = own_bands[m]
                    out[:, o * LANES : (o + 1) * LANES] = part
                else:
                    gsend[q, m] = part
        for q in range(max(q_from, 1), q_to):

            @pl.when(exists[q])
            def _():
                for m in range(m_from, m_to):
                    piece_copy(q, m).start()

    def wait_tiles(q, group):
        @pl.when(exists[q])
        def _():
            arrival(q, group).wait_recv()

    pltpu.make_async_copy(xbuf.at[0:ROW_SLOTS], xbuf.at[0:ROW_SLOTS], xsem.at[0]).wait()
    lax.fori_loop(0, BLOCKS, spread_own, 0)
    smooth_half(0, 0)
    smooth_half(0, 1)
    finish(0)

    pl.semaphore_wait(barrier, near_count)
    for group in range(2):
        for q in (3, 4, 1, 2):

            @pl.when(exists[q])
            def _():
                tile_copy(q, group).start()

    for q in range(1, NEAR):

        @pl.when(jnp.logical_not(exists[q]))
        def _():
            tpack[q] = jnp.zeros((2, 2, FINE, LANES), F32)

    for o in range(OFFSETS):
        if o not in own_bands:
            out[:, o * LANES : (o + 1) * LANES] = jnp.zeros((LANES, LANES), F32)

    pltpu.make_async_copy(xbuf.at[ROW_SLOTS:SLOTS], xbuf.at[ROW_SLOTS:SLOTS], xsem.at[1]).wait()
    lax.fori_loop(0, BLOCKS, spread_near, 0)

    for q in (1, 2):
        for group in range(2):
            wait_tiles(q, group)
            smooth_half(q, group)
        finish(q)
    for group in range(2):
        for q in (3, 4):
            wait_tiles(q, group)
            smooth_half(q, group)
    finish(3)
    finish(4)
    make_and_send(3, 5, 0, 2)
    make_and_send(3, 5, 2, 4)
    make_and_send(3, 5, 4, 5)
    make_and_send(1, 3, 0, 2)
    make_and_send(1, 3, 2, 4)
    make_and_send(1, 3, 4, 5)
    make_and_send(0, 1, 0, 5)
    for m in range(NEAR):
        for q in (1, 2, 3, 4):

            @pl.when(exists[q])
            def _():
                piece_arrival(q, m).wait_recv()
                o = band_of(q, m)
                out[:, o * LANES : (o + 1) * LANES] += grecv[q, m]

    for q in range(1, NEAR):

        @pl.when(exists[q])
        def _():
            for group in range(2):
                tile_copy(q, group).wait_send()
            for m in range(NEAR):
                piece_copy(q, m).wait_send()


def solution(mesh):
    rows, cols = mesh.shape["row"], mesh.shape["col"]

    def body(stiffness_blocks, block_columns, block_counts, tentative_tiles, aggregate_of):
        any_spec = pl.BlockSpec(memory_space=pl.ANY)
        in_hbm = lambda x: pltpu.with_memory_space_constraint(x, pltpu.HBM)
        dma = pltpu.SemaphoreType.DMA
        result = pl.pallas_call(
            lambda *refs: kernel(rows, cols, *refs),
            out_shape=jax.ShapeDtypeStruct((2 * FINE, OFFSETS * LANES), F32),
            in_specs=[any_spec] * 5,
            out_specs=pl.BlockSpec(memory_space=pltpu.VMEM),
            scratch_shapes=[
                pltpu.SMEM((BLOCKS, SLOTS), jnp.int32),
                pltpu.SMEM((BLOCKS, NEAR), jnp.int32),
                pltpu.SMEM(aggregate_of.shape, jnp.int32),
                pltpu.VMEM((SLOTS, BLOCKS, CHUNKS, LANES), F32),
                pltpu.VMEM((NEAR, 2, 8, CHUNKS, LANES), BF16),
                pltpu.VMEM((NEAR, 2, 2 * BLOCKS * CHUNKS, 4 * LANES), BF16),
                pltpu.SMEM((NEAR, BLOCKS), jnp.int32),
                pltpu.VMEM((BLOCKS, CHUNKS, LANES), F32),
                pltpu.VMEM((NEAR, 2, 2, FINE, LANES), F32),
                pltpu.VMEM((2, 4 * LANES, 2 * LANES), BF16),
                pltpu.VMEM((NEAR, 2, BLOCKS * CHUNKS, LANES), F32),
                pltpu.VMEM((2, BLOCKS * CHUNKS, LANES), F32),
                pltpu.VMEM((2, BLOCKS * FINE, NEAR * LANES), BF16),
                pltpu.VMEM((2, NEAR * LANES, BLOCKS * FINE), BF16),
                pltpu.VMEM((NEAR, NEAR, LANES, LANES), F32),
                pltpu.VMEM((NEAR, NEAR, LANES, LANES), F32),
                dma((2,)),
                dma,
                dma((3,)),
                dma((NEAR, 2)),
                dma((NEAR, 2)),
                dma((NEAR, NEAR)),
                dma((NEAR, NEAR)),
            ],
            compiler_params=pltpu.CompilerParams(
                collective_id=0, has_side_effects=True, vmem_limit_bytes=40 << 20
            ),
        )(
            in_hbm(jnp.transpose(stiffness_blocks, (1, 0, 2))),
            in_hbm(block_columns),
            in_hbm(block_counts),
            in_hbm(tentative_tiles),
            in_hbm(aggregate_of),
        )
        return result.reshape(2, FINE, OFFSETS * LANES)

    by_device = P(("row", "col"), None)
    by_device3 = P(("row", "col"), None, None)
    return jax.shard_map(
        body,
        mesh=mesh,
        in_specs=(by_device3, by_device, by_device, by_device, P()),
        out_specs=by_device3,
        check_vma=False,
    )
```

```python
import jax
import jax.numpy as jnp
from jax import lax
from jax.experimental import pallas as pl
from jax.experimental.pallas import tpu as pltpu
from jax.sharding import PartitionSpec as P

MESH = pl.DeviceIdType.MESH
F32 = jnp.float32
BF16 = jnp.bfloat16

FINE = 64
BLOCKS = 8
SLOTS = 20
ROW_SLOTS = 4
CHUNKS = 32
LANES = 128
OMEGA = 2.0 / 3.0

ROW_STEPS = (0, 1, -1, 0, 0)
COL_STEPS = (0, 0, 0, -1, 1)
OPPOSITE = (0, 1, 2, 4, 3)
OFFSETS = 13
NEAR = 5


def dot(a, b):
    return jnp.dot(a, b, preferred_element_type=F32)


def split(x):
    high = x.astype(BF16)
    return high, (x - high.astype(F32)).astype(BF16)


def kernel(
    rows,
    cols,
    stiff,
    columns_in,
    counts_in,
    tiles,
    aggs_in,
    out,
    columns,
    counts,
    aggs,
    xbuf,
    compact,
    dense,
    order,
    tp,
    tpack,
    weights,
    halves,
    damp,
    right,
    left,
    gsend,
    grecv,
    xsem,
    tsem,
    ssem,
    tsend,
    trecv,
    gsend_sem,
    grecv_sem,
):
    my_row = lax.axis_index("row")
    my_col = lax.axis_index("col")
    even = lax.rem(my_row, 2) == 0
    sign = jnp.where(even, 1, -1)
    places = [(my_row + sign * ROW_STEPS[q], my_col + COL_STEPS[q]) for q in range(NEAR)]
    exists = [
        True,
        True,
        (places[2][0] >= 0) & (places[2][0] < rows),
        my_col > 0,
        my_col < cols - 1,
    ]
    first_slots = [
        0,
        jnp.where(even, 16, 12),
        jnp.where(even, 12, 16),
        4,
        8,
    ]

    def band(row_units, col_step):
        if row_units == 0:
            return 6 + col_step
        ahead, behind = {1: (10, 2), -1: (2, 10), 2: (12, 0), -2: (0, 12)}[row_units]
        return jnp.where(even, ahead, behind) + col_step

    def band_of(q, m):
        turn = -1 if q in (1, 2) else 1
        return band(ROW_STEPS[q] + turn * ROW_STEPS[m], COL_STEPS[q] + COL_STEPS[m])

    def lanes_of(o):
        if isinstance(o, int):
            return slice(o * LANES, (o + 1) * LANES)
        return pl.ds(pl.multiple_of(o * LANES, LANES), LANES)

    def when_there(q):
        def run(f):
            if exists[q] is True:
                f()
            else:
                pl.when(exists[q])(f)

        return run

    barrier = pltpu.get_barrier_semaphore()
    near_count = jnp.int32(1)
    for q in range(1, NEAR):
        if q > 1:
            near_count = near_count + jnp.where(exists[q], 1, 0)

        @when_there(q)
        def _():
            pl.semaphore_signal(barrier, inc=1, device_id=places[q], device_id_type=MESH)

    for i in range(CHUNKS):
        pltpu.make_async_copy(tiles.at[:, pl.ds(i * LANES, LANES)], tp.at[:, i, :], tsem).start()
    small = [
        pltpu.make_async_copy(columns_in, columns, ssem.at[0]),
        pltpu.make_async_copy(counts_in, counts, ssem.at[1]),
        pltpu.make_async_copy(aggs_in, aggs, ssem.at[2]),
    ]
    for copy in small:
        copy.start()
    for first, last, sem in ((0, ROW_SLOTS, xsem.at[0]), (ROW_SLOTS, SLOTS, xsem.at[1])):
        for i in range(CHUNKS):
            pltpu.make_async_copy(
                stiff.at[first:last, :, pl.ds(i * LANES, LANES)], xbuf.at[first:last, :, i, :], sem
            ).start()

    lane = lax.broadcasted_iota(jnp.int32, (1, LANES), 1)
    low_half = lane < FINE

    for copy in small:
        copy.wait()
    own_groups = None
    for q in range(NEAR):
        near_row = jnp.clip(places[q][0], 0, rows - 1)
        near_col = jnp.clip(places[q][1], 0, cols - 1)
        first = (near_row * cols + near_col) * BLOCKS
        groups = [aggs[first + j] & 1 for j in range(BLOCKS)]
        word = jnp.int32(0)
        ones = jnp.int32(0)
        for j in range(BLOCKS):
            at = jnp.where(groups[j] == 1, 4 + ones, j - ones)
            word = word | (jnp.int32(j) << (4 * at))
            ones = ones + groups[j]
        if q == 0:
            own_groups = groups
        for n in range(BLOCKS):
            order[q, n] = (word >> (4 * n)) & 7

    pltpu.make_async_copy(tp, tp, tsem).wait()
    for group in range(2):
        for pair in range(2):
            a = tp[order[0, 4 * group + 2 * pair]]
            b = tp[order[0, 4 * group + 2 * pair + 1]]
            tpack[0, group, pair, pl.ds(0, CHUNKS, 2), :] = jnp.where(low_half, a, pltpu.roll(b, FINE, 1))
            tpack[0, group, pair, pl.ds(1, CHUNKS, 2), :] = jnp.where(low_half, pltpu.roll(a, FINE, 1), b)

    def tile_copy(q, group):
        return pltpu.make_async_remote_copy(
            src_ref=tpack.at[0, group],
            dst_ref=tpack.at[OPPOSITE[q], group],
            send_sem=tsend.at[q, group],
            recv_sem=trecv.at[OPPOSITE[q], group],
            device_id=places[q],
            device_id_type=MESH,
        )

    def arrival(q, group):
        return pltpu.make_async_remote_copy(
            src_ref=tpack.at[0, group],
            dst_ref=tpack.at[q, group],
            send_sem=tsend.at[q, group],
            recv_sem=trecv.at[q, group],
            device_id=places[q],
            device_id_type=MESH,
        )

    row_at = lax.broadcasted_iota(jnp.int32, (CHUNKS, LANES), 0)
    lane_at = lax.broadcasted_iota(jnp.int32, (CHUNKS, LANES), 1)

    zero = jnp.zeros((CHUNKS, LANES), BF16)
    for q in range(NEAR):
        compact[q, 0, 0] = zero
        compact[q, 1, 0] = zero

    def spread(q, k):
        slots = first_slots[q]
        rows_k = pl.ds(pl.multiple_of(k * CHUNKS, CHUNKS), CHUNKS)
        rows_low = pl.ds(pl.multiple_of(k * CHUNKS + 256, CHUNKS), CHUNKS)
        count = counts[k, slots // ROW_SLOTS]
        word = jnp.int32(0)
        for t in range(ROW_SLOTS):
            high, low = split(xbuf[slots + t, k])
            compact[q, 0, t + 1] = high
            compact[q, 1, t + 1] = low
            word = word | jnp.where(t < count, (t + 1) << (columns[k, slots + t] * 4), 0)
        for group in range(2):
            for n in range(4):
                e = (word >> (4 * order[q, 4 * group + n])) & 7
                lanes_n = slice(n * LANES, (n + 1) * LANES)
                dense[q, group, rows_k, lanes_n] = compact[q, 0, e]
                dense[q, group, rows_low, lanes_n] = compact[q, 1, e]

    def spread_own(k, _):
        x0 = xbuf[0, k]
        diagonal = [
            jnp.sum(
                jnp.where(lane_at == 2 * row_at + p * (FINE + 1), x0, 0.0), axis=1, keepdims=True
            )
            for p in range(2)
        ]
        rows_k = pl.ds(pl.multiple_of(k * CHUNKS, CHUNKS), CHUNKS)
        damp[rows_k, :] = OMEGA / jnp.where(low_half, diagonal[0], diagonal[1])
        spread(0, k)
        return 0

    def spread_near(k, _):
        for q in range(1, NEAR):
            spread(q, k)
        return 0

    def smooth_half(q, group):
        for pair in range(2):
            v = tpack[q, group, pair]
            r = pltpu.roll(v, FINE, 1)
            for part, (v_part, r_part) in enumerate(zip(split(v), split(r))):
                lanes_part = slice(part * LANES, (part + 1) * LANES)
                none = jnp.zeros_like(v_part)
                tiles_at = (
                    jnp.where(low_half, v_part, none),
                    jnp.where(low_half, none, r_part),
                    jnp.where(low_half, r_part, none),
                    jnp.where(low_half, none, v_part),
                )
                for n in range(4):
                    rows_n = slice((4 * pair + n) * FINE, (4 * pair + n + 1) * FINE)
                    weights[q, group, rows_n, lanes_part] = tiles_at[n]
        x = dot(dense[q, group, :256], weights[q, group])
        y = dot(dense[q, group, 256:], weights[q, group, :, :LANES])
        s = x[:, :LANES] + (x[:, LANES:] + y)
        halves[q, group] = s
        l = -(damp[...] * s)
        if q == 0:
            own = [jnp.where(own_groups[k] == group, tp[k], 0.0) for k in range(BLOCKS)]
            l = l + jnp.concatenate(own, axis=0)
        first = q * LANES + group * FINE
        for part, l_part in enumerate(split(l.T)):
            for p in range(2):
                left[part, first : first + FINE, p * 256 : (p + 1) * 256] = l_part[p * FINE : (p + 1) * FINE]

    def make_right(q):
        s_0, s_1 = halves[q, 0], halves[q, 1]
        by_parity = (
            jnp.where(low_half, s_0, pltpu.roll(s_1, FINE, 1)),
            jnp.where(low_half, pltpu.roll(s_0, FINE, 1), s_1),
        )
        for p in range(2):
            for part, r_part in enumerate(split(by_parity[p])):
                right[part, p * 256 : (p + 1) * 256, lanes_of(q)] = r_part

    def smooth(q):
        smooth_half(q, 0)
        smooth_half(q, 1)
        make_right(q)

    def products(row_list, m_from, m_to):
        cols_r = slice(m_from * LANES, m_to * LANES)
        highs = jnp.concatenate([left[0, a : a + n, :] for a, n in row_list], axis=0)
        lows = jnp.concatenate([left[1, a : a + n, :] for a, n in row_list], axis=0)
        return (
            dot(highs, right[0, :, cols_r])
            + dot(lows, right[0, :, cols_r])
            + dot(highs, right[1, :, cols_r])
        )

    def piece(q, m, group, to):
        at = pl.ds(0, LANES) if group is None else pl.ds(group * FINE, FINE)
        spot = group or 0
        return pltpu.make_async_remote_copy(
            src_ref=gsend.at[q, m, at],
            dst_ref=grecv.at[to, m, at],
            send_sem=gsend_sem.at[q, m, spot],
            recv_sem=grecv_sem.at[to, m, spot],
            device_id=places[q],
            device_id_type=MESH,
        )

    def piece_copy(q, m, group):
        return piece(q, m, group, OPPOSITE[q])

    def piece_arrival(q, m, group):
        return piece(q, m, group, q)

    def start_pieces(q, m_from, m_to, group):
        @when_there(q)
        def _():
            for m in range(m_from, m_to):
                piece_copy(q, m, group).start()

    def make_and_send(q_list, m_from, m_to):
        g = products([(q * LANES, LANES) for q in q_list], m_from, m_to)
        for at, q in enumerate(q_list):
            for m in range(m_from, m_to):
                part = g[at * LANES : (at + 1) * LANES, (m - m_from) * LANES : (m - m_from + 1) * LANES]
                if q == 0:
                    out[:, lanes_of(band_of(0, m))] = part
                else:
                    gsend[q, m] = part
        for q in q_list:
            if q > 0:
                start_pieces(q, m_from, m_to, None)

    def make_and_send_halves(group, m_from, m_to):
        g = products([(q * LANES + group * FINE, FINE) for q in (3, 4)], m_from, m_to)
        for at, q in enumerate((3, 4)):
            for m in range(m_from, m_to):
                gsend[q, m, group * FINE : (group + 1) * FINE] = g[
                    at * FINE : (at + 1) * FINE, (m - m_from) * LANES : (m - m_from + 1) * LANES
                ]
        for q in (3, 4):
            start_pieces(q, m_from, m_to, group)

    def wait_tiles(q, group):
        @when_there(q)
        def _():
            arrival(q, group).wait_recv()

    pl.semaphore_wait(barrier, near_count)
    for group in range(2):
        for q in (3, 4, 2, 1):

            @when_there(q)
            def _():
                tile_copy(q, group).start()

    for q in range(2, NEAR):

        @pl.when(jnp.logical_not(exists[q]))
        def _():
            tpack[q] = jnp.zeros((2, 2, FINE, LANES), F32)

    for o in range(OFFSETS):
        if o not in (2, 5, 6, 7, 10):
            out[:, lanes_of(o)] = jnp.zeros((LANES, LANES), F32)

    pltpu.make_async_copy(xbuf.at[0:ROW_SLOTS], xbuf.at[0:ROW_SLOTS], xsem.at[0]).wait()
    lax.fori_loop(0, BLOCKS, spread_own, 0)
    pltpu.make_async_copy(xbuf.at[ROW_SLOTS:SLOTS], xbuf.at[ROW_SLOTS:SLOTS], xsem.at[1]).wait()
    lax.fori_loop(0, BLOCKS, spread_near, 0)
    smooth(0)
    wait_tiles(1, 0)
    wait_tiles(1, 1)
    smooth(1)
    make_and_send((1,), 0, 2)
    make_and_send((0,), 0, 2)
    for group in range(2):
        wait_tiles(3, group)
        wait_tiles(4, group)
        smooth_half(3, group)
        smooth_half(4, group)
        make_and_send_halves(group, 0, 2)
    wait_tiles(2, 0)
    wait_tiles(2, 1)
    smooth(2)
    make_and_send((2,), 0, 2)
    make_right(3)
    make_right(4)
    make_and_send((3, 4), 2, 4)
    make_and_send((3, 4), 4, 5)
    make_and_send((2,), 2, 5)
    make_and_send((1,), 2, 5)
    make_and_send((0,), 2, 5)

    def groups_of(q, m):
        return (0, 1) if q in (3, 4) and m < 2 else (None,)

    for q_list, m_list in (((1,), (0, 1)), ((3, 4), (0, 1)), ((1,), (2, 3, 4)), ((2, 3, 4), (2, 3)), ((2,), (0, 1)), ((2, 3, 4), (4,))):
        for m in m_list:
            for q in q_list:

                @when_there(q)
                def _():
                    for group in groups_of(q, m):
                        piece_arrival(q, m, group).wait_recv()
                    out[:, lanes_of(band_of(q, m))] += grecv[q, m]

    for q in range(1, NEAR):

        @when_there(q)
        def _():
            for group in range(2):
                tile_copy(q, group).wait_send()
            for m in range(NEAR):
                for group in groups_of(q, m):
                    piece_copy(q, m, group).wait_send()


def solution(mesh):
    rows, cols = mesh.shape["row"], mesh.shape["col"]

    def body(stiffness_blocks, block_columns, block_counts, tentative_tiles, aggregate_of):
        any_spec = pl.BlockSpec(memory_space=pl.ANY)
        in_hbm = lambda x: pltpu.with_memory_space_constraint(x, pltpu.HBM)
        dma = pltpu.SemaphoreType.DMA
        result = pl.pallas_call(
            lambda *refs: kernel(rows, cols, *refs),
            out_shape=jax.ShapeDtypeStruct((2 * FINE, OFFSETS * LANES), F32),
            in_specs=[any_spec] * 5,
            out_specs=pl.BlockSpec(memory_space=pltpu.VMEM),
            scratch_shapes=[
                pltpu.SMEM((BLOCKS, SLOTS), jnp.int32),
                pltpu.SMEM((BLOCKS, NEAR), jnp.int32),
                pltpu.SMEM(aggregate_of.shape, jnp.int32),
                pltpu.VMEM((SLOTS, BLOCKS, CHUNKS, LANES), F32),
                pltpu.VMEM((NEAR, 2, 8, CHUNKS, LANES), BF16),
                pltpu.VMEM((NEAR, 2, 2 * BLOCKS * CHUNKS, 4 * LANES), BF16),
                pltpu.SMEM((NEAR, BLOCKS), jnp.int32),
                pltpu.VMEM((BLOCKS, CHUNKS, LANES), F32),
                pltpu.VMEM((NEAR, 2, 2, FINE, LANES), F32),
                pltpu.VMEM((NEAR, 2, 4 * LANES, 2 * LANES), BF16),
                pltpu.VMEM((NEAR, 2, BLOCKS * CHUNKS, LANES), F32),
                pltpu.VMEM((BLOCKS * CHUNKS, LANES), F32),
                pltpu.VMEM((2, BLOCKS * FINE, NEAR * LANES), BF16),
                pltpu.VMEM((2, NEAR * LANES, BLOCKS * FINE), BF16),
                pltpu.VMEM((NEAR, NEAR, LANES, LANES), F32),
                pltpu.VMEM((NEAR, NEAR, LANES, LANES), F32),
                dma((2,)),
                dma,
                dma((3,)),
                dma((NEAR, 2)),
                dma((NEAR, 2)),
                dma((NEAR, NEAR, 2)),
                dma((NEAR, NEAR, 2)),
            ],
            compiler_params=pltpu.CompilerParams(
                collective_id=0, has_side_effects=True, vmem_limit_bytes=40 << 20
            ),
        )(
            in_hbm(jnp.transpose(stiffness_blocks, (1, 0, 2))),
            in_hbm(block_columns),
            in_hbm(block_counts),
            in_hbm(tentative_tiles),
            in_hbm(aggregate_of),
        )
        return result.reshape(2, FINE, OFFSETS * LANES)

    by_device = P(("row", "col"), None)
    by_device3 = P(("row", "col"), None, None)
    return jax.shard_map(
        body,
        mesh=mesh,
        in_specs=(by_device3, by_device, by_device, by_device, P()),
        out_specs=by_device3,
        check_vma=False,
    )
```

```python
import jax
import jax.numpy as jnp
from jax import lax
from jax.experimental import pallas as pl
from jax.experimental.pallas import tpu as pltpu
from jax.sharding import PartitionSpec as P

MESH = pl.DeviceIdType.MESH
F32 = jnp.float32
BF16 = jnp.bfloat16

FINE = 64
BLOCKS = 8
SLOTS = 20
ROW_SLOTS = 4
CHUNKS = 32
LANES = 128
OMEGA = 2.0 / 3.0

ROW_STEPS = (0, 1, -1, 0, 0)
COL_STEPS = (0, 0, 0, -1, 1)
OPPOSITE = (0, 1, 2, 4, 3)
OFFSETS = 13
NEAR = 5
X_CHIPS = 4


def dot(a, b):
    return jnp.dot(a, b, preferred_element_type=F32)


def split(x):
    high = x.astype(BF16)
    return high, (x - high.astype(F32)).astype(BF16)


def kernel(
    rows,
    cols,
    stiff,
    columns_in,
    counts_in,
    tiles,
    aggs_in,
    out,
    columns,
    counts,
    aggs,
    xbuf,
    compact,
    dense,
    order,
    tp,
    tpack,
    weights,
    halves,
    damp,
    right,
    left,
    gsend,
    grecv,
    xsem,
    tsem,
    ssem,
    tsend,
    trecv,
    gsend_sem,
    grecv_sem,
):
    my_row = lax.axis_index("row")
    my_col = lax.axis_index("col")
    even = lax.rem(my_row, 2) == 0
    sign = jnp.where(even, 1, -1)
    places = [(my_row + sign * ROW_STEPS[q], my_col + COL_STEPS[q]) for q in range(NEAR)]
    exists = [
        True,
        True,
        (places[2][0] >= 0) & (places[2][0] < rows),
        my_col > 0,
        my_col < cols - 1,
    ]
    first_slots = [
        0,
        jnp.where(even, 16, 12),
        jnp.where(even, 12, 16),
        4,
        8,
    ]

    def band(row_units, col_step):
        if row_units == 0:
            return 6 + col_step
        ahead, behind = {1: (10, 2), -1: (2, 10), 2: (12, 0), -2: (0, 12)}[row_units]
        return jnp.where(even, ahead, behind) + col_step

    def band_of(q, m):
        turn = -1 if q in (1, 2) else 1
        return band(ROW_STEPS[q] + turn * ROW_STEPS[m], COL_STEPS[q] + COL_STEPS[m])

    def lanes_of(o):
        if isinstance(o, int):
            return slice(o * LANES, (o + 1) * LANES)
        return pl.ds(pl.multiple_of(o * LANES, LANES), LANES)

    def when_there(q):
        def run(f):
            if exists[q] is True:
                f()
            else:
                pl.when(exists[q])(f)

        return run

    left_far = lax.rem(my_col, X_CHIPS) == 0

    barrier = pltpu.get_barrier_semaphore()
    near_count = jnp.int32(1)
    for q in range(1, NEAR):
        if q > 1:
            near_count = near_count + jnp.where(exists[q], 1, 0)

        @when_there(q)
        def _():
            pl.semaphore_signal(barrier, inc=1, device_id=places[q], device_id_type=MESH)

    for i in range(CHUNKS):
        pltpu.make_async_copy(tiles.at[:, pl.ds(i * LANES, LANES)], tp.at[:, i, :], tsem).start()
    small = [
        pltpu.make_async_copy(columns_in, columns, ssem.at[0]),
        pltpu.make_async_copy(counts_in, counts, ssem.at[1]),
        pltpu.make_async_copy(aggs_in, aggs, ssem.at[2]),
    ]
    for copy in small:
        copy.start()
    for first, last, sem in ((0, ROW_SLOTS, xsem.at[0]), (ROW_SLOTS, SLOTS, xsem.at[1])):
        for i in range(CHUNKS):
            pltpu.make_async_copy(
                stiff.at[first:last, :, pl.ds(i * LANES, LANES)], xbuf.at[first:last, :, i, :], sem
            ).start()

    lane = lax.broadcasted_iota(jnp.int32, (1, LANES), 1)
    low_half = lane < FINE

    for copy in small:
        copy.wait()
    own_groups = None
    for q in range(NEAR):
        near_row = jnp.clip(places[q][0], 0, rows - 1)
        near_col = jnp.clip(places[q][1], 0, cols - 1)
        first = (near_row * cols + near_col) * BLOCKS
        groups = [aggs[first + j] & 1 for j in range(BLOCKS)]
        word = jnp.int32(0)
        ones = jnp.int32(0)
        for j in range(BLOCKS):
            at = jnp.where(groups[j] == 1, 4 + ones, j - ones)
            word = word | (jnp.int32(j) << (4 * at))
            ones = ones + groups[j]
        if q == 0:
            own_groups = groups
        for n in range(BLOCKS):
            order[q, n] = (word >> (4 * n)) & 7

    pltpu.make_async_copy(tp, tp, tsem).wait()
    for group in range(2):
        for pair in range(2):
            a = tp[order[0, 4 * group + 2 * pair]]
            b = tp[order[0, 4 * group + 2 * pair + 1]]
            tpack[0, group, pair, pl.ds(0, CHUNKS, 2), :] = jnp.where(low_half, a, pltpu.roll(b, FINE, 1))
            tpack[0, group, pair, pl.ds(1, CHUNKS, 2), :] = jnp.where(low_half, pltpu.roll(a, FINE, 1), b)

    def tile_copy(q, group):
        return pltpu.make_async_remote_copy(
            src_ref=tpack.at[0, group],
            dst_ref=tpack.at[OPPOSITE[q], group],
            send_sem=tsend.at[q - 1],
            recv_sem=trecv.at[OPPOSITE[q] - 1, group],
            device_id=places[q],
            device_id_type=MESH,
        )

    def arrival(q, group):
        return pltpu.make_async_remote_copy(
            src_ref=tpack.at[0, group],
            dst_ref=tpack.at[q, group],
            send_sem=tsend.at[q - 1],
            recv_sem=trecv.at[q - 1, group],
            device_id=places[q],
            device_id_type=MESH,
        )

    row_at = lax.broadcasted_iota(jnp.int32, (CHUNKS, LANES), 0)
    lane_at = lax.broadcasted_iota(jnp.int32, (CHUNKS, LANES), 1)

    zero = jnp.zeros((CHUNKS, LANES), BF16)
    for q in range(NEAR):
        compact[q, 0, 0] = zero
        compact[q, 1, 0] = zero

    def spread(q, k):
        slots = first_slots[q]
        rows_k = pl.ds(pl.multiple_of(k * CHUNKS, CHUNKS), CHUNKS)
        rows_low = pl.ds(pl.multiple_of(k * CHUNKS + 256, CHUNKS), CHUNKS)
        count = counts[k, slots // ROW_SLOTS]
        word = jnp.int32(0)
        for t in range(ROW_SLOTS):
            high, low = split(xbuf[slots + t, k])
            compact[q, 0, t + 1] = high
            compact[q, 1, t + 1] = low
            word = word | jnp.where(t < count, (t + 1) << (columns[k, slots + t] * 4), 0)
        for group in range(2):
            for n in range(4):
                e = (word >> (4 * order[q, 4 * group + n])) & 7
                lanes_n = slice(n * LANES, (n + 1) * LANES)
                dense[q, group, rows_k, lanes_n] = compact[q, 0, e]
                dense[q, group, rows_low, lanes_n] = compact[q, 1, e]

    def spread_own(k, _):
        x0 = xbuf[0, k]
        diagonal = [
            jnp.sum(
                jnp.where(lane_at == 2 * row_at + p * (FINE + 1), x0, 0.0), axis=1, keepdims=True
            )
            for p in range(2)
        ]
        rows_k = pl.ds(pl.multiple_of(k * CHUNKS, CHUNKS), CHUNKS)
        damp[rows_k, :] = OMEGA / jnp.where(low_half, diagonal[0], diagonal[1])
        spread(0, k)
        return 0

    def spread_near(k, _):
        for q in range(1, NEAR):
            spread(q, k)
        return 0

    def smooth_half(q, group):
        for pair in range(2):
            v = tpack[q, group, pair]
            r = pltpu.roll(v, FINE, 1)
            for part, (v_part, r_part) in enumerate(zip(split(v), split(r))):
                lanes_part = slice(part * LANES, (part + 1) * LANES)
                none = jnp.zeros_like(v_part)
                tiles_at = (
                    jnp.where(low_half, v_part, none),
                    jnp.where(low_half, none, r_part),
                    jnp.where(low_half, r_part, none),
                    jnp.where(low_half, none, v_part),
                )
                for n in range(4):
                    rows_n = slice((4 * pair + n) * FINE, (4 * pair + n + 1) * FINE)
                    weights[q, group, rows_n, lanes_part] = tiles_at[n]
        x = dot(dense[q, group, :256], weights[q, group])
        y = dot(dense[q, group, 256:], weights[q, group, :, :LANES])
        s = x[:, :LANES] + (x[:, LANES:] + y)
        halves[q, group] = s
        l = -(damp[...] * s)
        if q == 0:
            own = [jnp.where(own_groups[k] == group, tp[k], 0.0) for k in range(BLOCKS)]
            l = l + jnp.concatenate(own, axis=0)
        first = q * LANES + group * FINE
        for part, l_part in enumerate(split(l.T)):
            for p in range(2):
                left[part, first : first + FINE, p * 256 : (p + 1) * 256] = l_part[p * FINE : (p + 1) * FINE]

    def make_right(q):
        s_0, s_1 = halves[q, 0], halves[q, 1]
        by_parity = (
            jnp.where(low_half, s_0, pltpu.roll(s_1, FINE, 1)),
            jnp.where(low_half, pltpu.roll(s_0, FINE, 1), s_1),
        )
        for p in range(2):
            for part, r_part in enumerate(split(by_parity[p])):
                right[part, p * 256 : (p + 1) * 256, lanes_of(q)] = r_part

    def smooth(q):
        smooth_half(q, 0)
        smooth_half(q, 1)
        make_right(q)

    def products(row_list, m_from, m_to):
        cols_r = slice(m_from * LANES, m_to * LANES)
        highs = jnp.concatenate([left[0, a : a + n, :] for a, n in row_list], axis=0)
        lows = jnp.concatenate([left[1, a : a + n, :] for a, n in row_list], axis=0)
        return (
            dot(highs, right[0, :, cols_r])
            + dot(lows, right[0, :, cols_r])
            + dot(highs, right[1, :, cols_r])
        )

    def piece_copy(q, m, group):
        at = pl.ds(0, LANES) if group is None else pl.ds(group * FINE, FINE)
        return pltpu.make_async_remote_copy(
            src_ref=gsend.at[q, m, at],
            dst_ref=grecv.at[OPPOSITE[q], m, at],
            send_sem=gsend_sem.at[q - 1],
            recv_sem=grecv_sem.at[OPPOSITE[q] - 1, m // 2],
            device_id=places[q],
            device_id_type=MESH,
        )

    def set_arrival(q, m_from, m_to):
        return pltpu.make_async_remote_copy(
            src_ref=gsend.at[q, m_from:m_to],
            dst_ref=grecv.at[q, m_from:m_to],
            send_sem=gsend_sem.at[q - 1],
            recv_sem=grecv_sem.at[q - 1, m_from // 2],
            device_id=places[q],
            device_id_type=MESH,
        )

    def all_sent(q):
        pltpu.make_async_remote_copy(
            src_ref=tpack.at[0],
            dst_ref=tpack.at[OPPOSITE[q]],
            send_sem=tsend.at[q - 1],
            recv_sem=trecv.at[q - 1, 0],
            device_id=places[q],
            device_id_type=MESH,
        ).wait_send()
        set_arrival(q, 0, NEAR).wait_send()

    def start_pieces(q, m_from, m_to, group):
        @when_there(q)
        def _():
            for m in range(m_from, m_to):
                piece_copy(q, m, group).start()

    def make_and_send(q_list, m_from, m_to):
        g = products([(q * LANES, LANES) for q in q_list], m_from, m_to)
        for at, q in enumerate(q_list):
            for m in range(m_from, m_to):
                part = g[at * LANES : (at + 1) * LANES, (m - m_from) * LANES : (m - m_from + 1) * LANES]
                if q == 0:
                    out[:, lanes_of(band_of(0, m))] = part
                else:
                    gsend[q, m] = part
        if q_list == (3, 4):
            far_first(lambda q: start_pieces(q, m_from, m_to, None))
        else:
            for q in q_list:
                if q > 0:
                    start_pieces(q, m_from, m_to, None)

    def make_and_send_halves(group, m_from, m_to):
        g = products([(q * LANES + group * FINE, FINE) for q in (3, 4)], m_from, m_to)
        for at, q in enumerate((3, 4)):
            for m in range(m_from, m_to):
                gsend[q, m, group * FINE : (group + 1) * FINE] = g[
                    at * FINE : (at + 1) * FINE, (m - m_from) * LANES : (m - m_from + 1) * LANES
                ]
        far_first(lambda q: start_pieces(q, m_from, m_to, group))

    def wait_tiles(q, group):
        @when_there(q)
        def _():
            arrival(q, group).wait_recv()

    pl.semaphore_wait(barrier, near_count)
    def send_tiles(q, group):
        @when_there(q)
        def _():
            tile_copy(q, group).start()

    def far_first(send):
        @pl.when(left_far)
        def _():
            send(3)
            send(4)

        @pl.when(jnp.logical_not(left_far))
        def _():
            send(4)
            send(3)

    for group in range(2):
        far_first(lambda q: send_tiles(q, group))
        for q in (2, 1):
            send_tiles(q, group)

    for q in range(2, NEAR):

        @pl.when(jnp.logical_not(exists[q]))
        def _():
            tpack[q] = jnp.zeros((2, 2, FINE, LANES), F32)

    for o in range(OFFSETS):
        if o not in (2, 5, 6, 7, 10):
            out[:, lanes_of(o)] = jnp.zeros((LANES, LANES), F32)

    pltpu.make_async_copy(xbuf.at[0:ROW_SLOTS], xbuf.at[0:ROW_SLOTS], xsem.at[0]).wait()
    lax.fori_loop(0, BLOCKS, spread_own, 0)
    pltpu.make_async_copy(xbuf.at[ROW_SLOTS:SLOTS], xbuf.at[ROW_SLOTS:SLOTS], xsem.at[1]).wait()
    lax.fori_loop(0, BLOCKS, spread_near, 0)
    smooth(0)
    wait_tiles(1, 0)
    wait_tiles(1, 1)
    smooth(1)
    make_and_send((1,), 0, 2)
    make_and_send((0,), 0, 2)
    for group in range(2):
        wait_tiles(3, group)
        wait_tiles(4, group)
        smooth_half(3, group)
        smooth_half(4, group)
        make_and_send_halves(group, 0, 2)
    wait_tiles(2, 0)
    wait_tiles(2, 1)
    smooth(2)
    make_and_send((2,), 0, 2)
    make_right(3)
    make_right(4)
    make_and_send((3, 4), 2, 4)
    make_and_send((3, 4), 4, 5)
    make_and_send((2,), 2, 5)
    make_and_send((1,), 2, 5)
    make_and_send((0,), 2, 5)

    for q_list, m_from, m_to in (
        ((1,), 0, 2),
        ((3, 4), 0, 2),
        ((1,), 2, 4),
        ((1,), 4, 5),
        ((2,), 0, 2),
        ((3, 4), 2, 4),
        ((2,), 2, 4),
        ((2,), 4, 5),
        ((3, 4), 4, 5),
    ):
        for q in q_list:

            @when_there(q)
            def _():
                set_arrival(q, m_from, m_to).wait_recv()
                for m in range(m_from, m_to):
                    out[:, lanes_of(band_of(q, m))] += grecv[q, m]

    for q in range(1, NEAR):

        @when_there(q)
        def _():
            all_sent(q)


def solution(mesh):
    rows, cols = mesh.shape["row"], mesh.shape["col"]

    def body(stiffness_blocks, block_columns, block_counts, tentative_tiles, aggregate_of):
        any_spec = pl.BlockSpec(memory_space=pl.ANY)
        in_hbm = lambda x: pltpu.with_memory_space_constraint(x, pltpu.HBM)
        dma = pltpu.SemaphoreType.DMA
        result = pl.pallas_call(
            lambda *refs: kernel(rows, cols, *refs),
            out_shape=jax.ShapeDtypeStruct((2 * FINE, OFFSETS * LANES), F32),
            in_specs=[any_spec] * 5,
            out_specs=pl.BlockSpec(memory_space=pltpu.VMEM),
            scratch_shapes=[
                pltpu.SMEM((BLOCKS, SLOTS), jnp.int32),
                pltpu.SMEM((BLOCKS, NEAR), jnp.int32),
                pltpu.SMEM(aggregate_of.shape, jnp.int32),
                pltpu.VMEM((SLOTS, BLOCKS, CHUNKS, LANES), F32),
                pltpu.VMEM((NEAR, 2, 8, CHUNKS, LANES), BF16),
                pltpu.VMEM((NEAR, 2, 2 * BLOCKS * CHUNKS, 4 * LANES), BF16),
                pltpu.SMEM((NEAR, BLOCKS), jnp.int32),
                pltpu.VMEM((BLOCKS, CHUNKS, LANES), F32),
                pltpu.VMEM((NEAR, 2, 2, FINE, LANES), F32),
                pltpu.VMEM((NEAR, 2, 4 * LANES, 2 * LANES), BF16),
                pltpu.VMEM((NEAR, 2, BLOCKS * CHUNKS, LANES), F32),
                pltpu.VMEM((BLOCKS * CHUNKS, LANES), F32),
                pltpu.VMEM((2, BLOCKS * FINE, NEAR * LANES), BF16),
                pltpu.VMEM((2, NEAR * LANES, BLOCKS * FINE), BF16),
                pltpu.VMEM((NEAR, NEAR, LANES, LANES), F32),
                pltpu.VMEM((NEAR, NEAR, LANES, LANES), F32),
                dma((2,)),
                dma,
                dma((3,)),
                dma((NEAR - 1,)),
                dma((NEAR - 1, 2)),
                dma((NEAR - 1,)),
                dma((NEAR - 1, 3)),
            ],
            compiler_params=pltpu.CompilerParams(
                collective_id=0, has_side_effects=True, vmem_limit_bytes=40 << 20
            ),
        )(
            in_hbm(jnp.transpose(stiffness_blocks, (1, 0, 2))),
            in_hbm(block_columns),
            in_hbm(block_counts),
            in_hbm(tentative_tiles),
            in_hbm(aggregate_of),
        )
        return result.reshape(2, FINE, OFFSETS * LANES)

    by_device = P(("row", "col"), None)
    by_device3 = P(("row", "col"), None, None)
    return jax.shard_map(
        body,
        mesh=mesh,
        in_specs=(by_device3, by_device, by_device, by_device, P()),
        out_specs=by_device3,
        check_vma=False,
    )
```

```python
import jax
import jax.numpy as jnp
from jax import lax
from jax.experimental import pallas as pl
from jax.experimental.pallas import tpu as pltpu
from jax.sharding import PartitionSpec as P

MESH = pl.DeviceIdType.MESH
F32 = jnp.float32
BF16 = jnp.bfloat16

FINE = 64
BLOCKS = 8
SLOTS = 20
ROW_SLOTS = 4
CHUNKS = 32
LANES = 128
OMEGA = 2.0 / 3.0

ROW_STEPS = (0, 1, -1, 0, 0)
COL_STEPS = (0, 0, 0, -1, 1)
OPPOSITE = (0, 1, 2, 4, 3)
OFFSETS = 13
NEAR = 5
X_CHIPS = 4


def dot(a, b):
    return jnp.dot(a, b, preferred_element_type=F32)


def split(x):
    high = x.astype(BF16)
    return high, (x - high.astype(F32)).astype(BF16)


def kernel(
    rows,
    cols,
    stiff,
    columns_in,
    counts_in,
    tiles,
    aggs_in,
    out,
    columns,
    counts,
    aggs,
    xbuf,
    compact,
    dense,
    order,
    tp,
    tpack,
    weights,
    halves,
    damp,
    right,
    left,
    gsend,
    grecv,
    psend,
    precv,
    xsem,
    tsem,
    ssem,
    tsend,
    trecv,
    gsend_sem,
    psend_sem,
    grecv_sem,
):
    my_row = lax.axis_index("row")
    my_col = lax.axis_index("col")
    even = lax.rem(my_row, 2) == 0
    sign = jnp.where(even, 1, -1)
    places = [(my_row + sign * ROW_STEPS[q], my_col + COL_STEPS[q]) for q in range(NEAR)]
    exists = [
        True,
        True,
        (places[2][0] >= 0) & (places[2][0] < rows),
        my_col > 0,
        my_col < cols - 1,
    ]
    first_slots = [
        0,
        jnp.where(even, 16, 12),
        jnp.where(even, 12, 16),
        4,
        8,
    ]

    def band(row_units, col_step):
        if row_units == 0:
            return 6 + col_step
        ahead, behind = {1: (10, 2), -1: (2, 10), 2: (12, 0), -2: (0, 12)}[row_units]
        return jnp.where(even, ahead, behind) + col_step

    def band_of(q, m):
        turn = -1 if q in (1, 2) else 1
        return band(ROW_STEPS[q] + turn * ROW_STEPS[m], COL_STEPS[q] + COL_STEPS[m])

    def lanes_of(o):
        if isinstance(o, int):
            return slice(o * LANES, (o + 1) * LANES)
        return pl.ds(pl.multiple_of(o * LANES, LANES), LANES)

    def when_there(q):
        def run(f):
            if exists[q] is True:
                f()
            else:
                pl.when(exists[q])(f)

        return run

    left_far = lax.rem(my_col, X_CHIPS) == 0

    barrier = pltpu.get_barrier_semaphore()
    near_count = jnp.int32(1)
    for q in range(1, NEAR):
        if q > 1:
            near_count = near_count + jnp.where(exists[q], 1, 0)

        @when_there(q)
        def _():
            pl.semaphore_signal(barrier, inc=1, device_id=places[q], device_id_type=MESH)

    for i in range(CHUNKS):
        pltpu.make_async_copy(tiles.at[:, pl.ds(i * LANES, LANES)], tp.at[:, i, :], tsem).start()
    small = [
        pltpu.make_async_copy(columns_in, columns, ssem.at[0]),
        pltpu.make_async_copy(counts_in, counts, ssem.at[1]),
        pltpu.make_async_copy(aggs_in, aggs, ssem.at[2]),
    ]
    for copy in small:
        copy.start()
    for first, last, sem in ((0, ROW_SLOTS, xsem.at[0]), (ROW_SLOTS, SLOTS, xsem.at[1])):
        for i in range(CHUNKS):
            pltpu.make_async_copy(
                stiff.at[first:last, :, pl.ds(i * LANES, LANES)], xbuf.at[first:last, :, i, :], sem
            ).start()

    lane = lax.broadcasted_iota(jnp.int32, (1, LANES), 1)
    low_half = lane < FINE

    for copy in small:
        copy.wait()
    own_groups = None
    for q in range(NEAR):
        near_row = jnp.clip(places[q][0], 0, rows - 1)
        near_col = jnp.clip(places[q][1], 0, cols - 1)
        first = (near_row * cols + near_col) * BLOCKS
        groups = [aggs[first + j] & 1 for j in range(BLOCKS)]
        word = jnp.int32(0)
        ones = jnp.int32(0)
        for j in range(BLOCKS):
            at = jnp.where(groups[j] == 1, 4 + ones, j - ones)
            word = word | (jnp.int32(j) << (4 * at))
            ones = ones + groups[j]
        if q == 0:
            own_groups = groups
        for n in range(BLOCKS):
            order[q, n] = (word >> (4 * n)) & 7

    pltpu.make_async_copy(tp, tp, tsem).wait()
    for group in range(2):
        for pair in range(2):
            a = tp[order[0, 4 * group + 2 * pair]]
            b = tp[order[0, 4 * group + 2 * pair + 1]]
            tpack[0, group, pair, pl.ds(0, CHUNKS, 2), :] = jnp.where(low_half, a, pltpu.roll(b, FINE, 1))
            tpack[0, group, pair, pl.ds(1, CHUNKS, 2), :] = jnp.where(low_half, pltpu.roll(a, FINE, 1), b)

    def tile_copy(q, group):
        return pltpu.make_async_remote_copy(
            src_ref=tpack.at[0, group],
            dst_ref=tpack.at[OPPOSITE[q], group],
            send_sem=tsend.at[q - 1],
            recv_sem=trecv.at[OPPOSITE[q] - 1, group],
            device_id=places[q],
            device_id_type=MESH,
        )

    def arrival(q, group):
        return pltpu.make_async_remote_copy(
            src_ref=tpack.at[0, group],
            dst_ref=tpack.at[q, group],
            send_sem=tsend.at[q - 1],
            recv_sem=trecv.at[q - 1, group],
            device_id=places[q],
            device_id_type=MESH,
        )

    row_at = lax.broadcasted_iota(jnp.int32, (CHUNKS, LANES), 0)
    lane_at = lax.broadcasted_iota(jnp.int32, (CHUNKS, LANES), 1)

    zero = jnp.zeros((CHUNKS, LANES), BF16)
    for q in range(NEAR):
        compact[q, 0, 0] = zero
        compact[q, 1, 0] = zero

    def spread(q, k):
        slots = first_slots[q]
        rows_k = pl.ds(pl.multiple_of(k * CHUNKS, CHUNKS), CHUNKS)
        rows_low = pl.ds(pl.multiple_of(k * CHUNKS + 256, CHUNKS), CHUNKS)
        count = counts[k, slots // ROW_SLOTS]
        word = jnp.int32(0)
        for t in range(ROW_SLOTS):
            high, low = split(xbuf[slots + t, k])
            compact[q, 0, t + 1] = high
            compact[q, 1, t + 1] = low
            word = word | jnp.where(t < count, (t + 1) << (columns[k, slots + t] * 4), 0)
        for group in range(2):
            for n in range(4):
                e = (word >> (4 * order[q, 4 * group + n])) & 7
                lanes_n = slice(n * LANES, (n + 1) * LANES)
                dense[q, group, rows_k, lanes_n] = compact[q, 0, e]
                dense[q, group, rows_low, lanes_n] = compact[q, 1, e]

    def spread_own(k, _):
        x0 = xbuf[0, k]
        diagonal = [
            jnp.sum(
                jnp.where(lane_at == 2 * row_at + p * (FINE + 1), x0, 0.0), axis=1, keepdims=True
            )
            for p in range(2)
        ]
        rows_k = pl.ds(pl.multiple_of(k * CHUNKS, CHUNKS), CHUNKS)
        damp[rows_k, :] = OMEGA / jnp.where(low_half, diagonal[0], diagonal[1])
        spread(0, k)
        return 0

    def spread_near(k, _):
        for q in range(1, NEAR):
            spread(q, k)
        return 0

    def smooth_half(q, group):
        for pair in range(2):
            v = tpack[q, group, pair]
            r = pltpu.roll(v, FINE, 1)
            for part, (v_part, r_part) in enumerate(zip(split(v), split(r))):
                lanes_part = slice(part * LANES, (part + 1) * LANES)
                none = jnp.zeros_like(v_part)
                tiles_at = (
                    jnp.where(low_half, v_part, none),
                    jnp.where(low_half, none, r_part),
                    jnp.where(low_half, r_part, none),
                    jnp.where(low_half, none, v_part),
                )
                for n in range(4):
                    rows_n = slice((4 * pair + n) * FINE, (4 * pair + n + 1) * FINE)
                    weights[q, group, rows_n, lanes_part] = tiles_at[n]
        x = dot(dense[q, group, :256], weights[q, group])
        y = dot(dense[q, group, 256:], weights[q, group, :, :LANES])
        s = x[:, :LANES] + (x[:, LANES:] + y)
        halves[q, group] = s
        l = -(damp[...] * s)
        if q == 0:
            own = [jnp.where(own_groups[k] == group, tp[k], 0.0) for k in range(BLOCKS)]
            l = l + jnp.concatenate(own, axis=0)
        first = q * LANES + group * FINE
        for part, l_part in enumerate(split(l.T)):
            for p in range(2):
                left[part, first : first + FINE, p * 256 : (p + 1) * 256] = l_part[p * FINE : (p + 1) * FINE]

    def make_right(q):
        s_0, s_1 = halves[q, 0], halves[q, 1]
        by_parity = (
            jnp.where(low_half, s_0, pltpu.roll(s_1, FINE, 1)),
            jnp.where(low_half, pltpu.roll(s_0, FINE, 1), s_1),
        )
        for p in range(2):
            for part, r_part in enumerate(split(by_parity[p])):
                right[part, p * 256 : (p + 1) * 256, lanes_of(q)] = r_part

    def smooth(q):
        smooth_half(q, 0)
        smooth_half(q, 1)
        make_right(q)

    def products(row_list, m_from, m_to):
        cols_r = slice(m_from * LANES, m_to * LANES)
        highs = jnp.concatenate([left[0, a : a + n, :] for a, n in row_list], axis=0)
        lows = jnp.concatenate([left[1, a : a + n, :] for a, n in row_list], axis=0)
        return (
            dot(highs, right[0, :, cols_r])
            + dot(lows, right[0, :, cols_r])
            + dot(highs, right[1, :, cols_r])
        )

    square_row = lax.broadcasted_iota(jnp.int32, (FINE, FINE), 0)
    square_col = lax.broadcasted_iota(jnp.int32, (FINE, FINE), 1)

    def packed(g):
        a, b, c = g[:FINE, :FINE], g[:FINE, FINE:], g[FINE:, FINE:]
        square = jnp.where(square_row >= square_col, a, c)
        diagonal = jnp.sum(jnp.where(square_row == square_col, c, 0.0), axis=0, keepdims=True)
        top = jnp.concatenate([square, b], axis=1)
        last = jnp.broadcast_to(jnp.concatenate([diagonal, diagonal], axis=1), (8, LANES))
        return jnp.concatenate([top, last], axis=0)

    def unpacked(x):
        square, b = x[:FINE, :FINE], x[:FINE, FINE:]
        diagonal = x[FINE : FINE + 1, :FINE]
        turned = x[:FINE].T
        square_t, b_t = turned[:FINE], turned[FINE:]
        a = jnp.where(square_row >= square_col, square, square_t)
        c = jnp.where(square_row < square_col, square, square_t)
        c = jnp.where(square_row == square_col, diagonal, c)
        return jnp.concatenate(
            [jnp.concatenate([a, b], axis=1), jnp.concatenate([b_t, c], axis=1)], axis=0
        )

    def piece_copy(q, m, group):
        to = OPPOSITE[q]
        recv_sem = grecv_sem.at[to - 1, max(m - 1, 0)]
        if m == q and q > 2:
            return pltpu.make_async_remote_copy(
                src_ref=psend.at[q - 1],
                dst_ref=precv.at[to - 1],
                send_sem=psend_sem.at[q - 1],
                recv_sem=recv_sem,
                device_id=places[q],
                device_id_type=MESH,
            )
        at = pl.ds(0, LANES) if group is None else pl.ds(group * FINE, FINE)
        return pltpu.make_async_remote_copy(
            src_ref=gsend.at[q, m, at],
            dst_ref=grecv.at[to, m, at],
            send_sem=gsend_sem.at[q - 1],
            recv_sem=recv_sem,
            device_id=places[q],
            device_id_type=MESH,
        )

    def set_arrival(q, m_from, m_to):
        alone = m_from == OPPOSITE[q] and q > 2
        return pltpu.make_async_remote_copy(
            src_ref=psend.at[q - 1] if alone else gsend.at[q, m_from:m_to],
            dst_ref=precv.at[q - 1] if alone else grecv.at[q, m_from:m_to],
            send_sem=gsend_sem.at[q - 1],
            recv_sem=grecv_sem.at[q - 1, max(m_from - 1, 0)],
            device_id=places[q],
            device_id_type=MESH,
        )

    def all_sent(q):
        pltpu.make_async_remote_copy(
            src_ref=tpack.at[0],
            dst_ref=tpack.at[OPPOSITE[q]],
            send_sem=tsend.at[q - 1],
            recv_sem=trecv.at[q - 1, 0],
            device_id=places[q],
            device_id_type=MESH,
        ).wait_send()
        pltpu.make_async_remote_copy(
            src_ref=gsend.at[q, 0:4] if q > 2 else gsend.at[q],
            dst_ref=grecv.at[q, 0:4] if q > 2 else grecv.at[q],
            send_sem=gsend_sem.at[q - 1],
            recv_sem=grecv_sem.at[q - 1, 0],
            device_id=places[q],
            device_id_type=MESH,
        ).wait_send()
        if q > 2:
            piece_copy(q, q, None).wait_send()

    def start_pieces(q, m_from, m_to, group):
        @when_there(q)
        def _():
            for m in sorted(range(m_from, m_to), key=lambda m: m != q):
                piece_copy(q, m, group).start()

    def make_and_send(q_list, m_from, m_to):
        g = products([(q * LANES, LANES) for q in q_list], m_from, m_to)
        for at, q in enumerate(q_list):
            for m in range(m_from, m_to):
                part = g[at * LANES : (at + 1) * LANES, (m - m_from) * LANES : (m - m_from + 1) * LANES]
                if q == 0:
                    out[:, lanes_of(band_of(0, m))] = part
                elif m == q and q > 2:
                    psend[q - 1] = packed(part)
                else:
                    gsend[q, m] = part
        if q_list == (3, 4):
            far_first(lambda q: start_pieces(q, m_from, m_to, None))
        else:
            for q in q_list:
                if q > 0:
                    start_pieces(q, m_from, m_to, None)

    def make_and_send_halves(group, m_from, m_to):
        g = products([(q * LANES + group * FINE, FINE) for q in (3, 4)], m_from, m_to)
        for at, q in enumerate((3, 4)):
            for m in range(m_from, m_to):
                gsend[q, m, group * FINE : (group + 1) * FINE] = g[
                    at * FINE : (at + 1) * FINE, (m - m_from) * LANES : (m - m_from + 1) * LANES
                ]
        far_first(lambda q: start_pieces(q, m_from, m_to, group))

    def wait_tiles(q, group):
        @when_there(q)
        def _():
            arrival(q, group).wait_recv()

    pl.semaphore_wait(barrier, near_count)
    def send_tiles(q, group):
        @when_there(q)
        def _():
            tile_copy(q, group).start()

    def far_first(send):
        @pl.when(left_far)
        def _():
            send(3)
            send(4)

        @pl.when(jnp.logical_not(left_far))
        def _():
            send(4)
            send(3)

    for group in range(2):
        far_first(lambda q: send_tiles(q, group))
        for q in (2, 1):
            send_tiles(q, group)

    for q in range(2, NEAR):

        @pl.when(jnp.logical_not(exists[q]))
        def _():
            tpack[q] = jnp.zeros((2, 2, FINE, LANES), F32)

    for o in range(OFFSETS):
        if o not in (2, 5, 6, 7, 10):
            out[:, lanes_of(o)] = jnp.zeros((LANES, LANES), F32)

    pltpu.make_async_copy(xbuf.at[0:ROW_SLOTS], xbuf.at[0:ROW_SLOTS], xsem.at[0]).wait()
    lax.fori_loop(0, BLOCKS, spread_own, 0)
    pltpu.make_async_copy(xbuf.at[ROW_SLOTS:SLOTS], xbuf.at[ROW_SLOTS:SLOTS], xsem.at[1]).wait()
    lax.fori_loop(0, BLOCKS, spread_near, 0)
    smooth(0)
    wait_tiles(1, 0)
    wait_tiles(1, 1)
    smooth(1)
    make_and_send((1,), 0, 2)
    make_and_send((0,), 0, 2)
    for group in range(2):
        wait_tiles(3, group)
        wait_tiles(4, group)
        smooth_half(3, group)
        smooth_half(4, group)
        make_and_send_halves(group, 0, 2)
    wait_tiles(2, 0)
    wait_tiles(2, 1)
    smooth(2)
    make_and_send((2,), 0, 2)
    make_right(3)
    make_right(4)
    make_and_send((3, 4), 2, 5)
    make_and_send((2,), 2, 5)
    make_and_send((1,), 2, 5)
    make_and_send((0,), 2, 5)

    for q_list, m_from, m_to in (
        ((1,), 0, 2),
        ((3, 4), 0, 2),
        ((1,), 2, 3),
        ((1,), 3, 4),
        ((1,), 4, 5),
        ((2,), 0, 2),
        ((3, 4), 2, 3),
        ((2,), 2, 3),
        ((2,), 3, 4),
        ((2,), 4, 5),
        ((4,), 3, 4),
        ((3,), 4, 5),
        ((3,), 3, 4),
        ((4,), 4, 5),
    ):
        for q in q_list:

            @when_there(q)
            def _():
                set_arrival(q, m_from, m_to).wait_recv()
                for m in range(m_from, m_to):
                    o = lanes_of(band_of(q, m))
                    if q > 2 and m == OPPOSITE[q]:
                        out[:, o] += unpacked(precv[q - 1])
                    else:
                        out[:, o] += grecv[q, m]

    for q in range(1, NEAR):

        @when_there(q)
        def _():
            all_sent(q)


def solution(mesh):
    rows, cols = mesh.shape["row"], mesh.shape["col"]

    def body(stiffness_blocks, block_columns, block_counts, tentative_tiles, aggregate_of):
        any_spec = pl.BlockSpec(memory_space=pl.ANY)
        in_hbm = lambda x: pltpu.with_memory_space_constraint(x, pltpu.HBM)
        dma = pltpu.SemaphoreType.DMA
        result = pl.pallas_call(
            lambda *refs: kernel(rows, cols, *refs),
            out_shape=jax.ShapeDtypeStruct((2 * FINE, OFFSETS * LANES), F32),
            in_specs=[any_spec] * 5,
            out_specs=pl.BlockSpec(memory_space=pltpu.VMEM),
            scratch_shapes=[
                pltpu.SMEM((BLOCKS, SLOTS), jnp.int32),
                pltpu.SMEM((BLOCKS, NEAR), jnp.int32),
                pltpu.SMEM(aggregate_of.shape, jnp.int32),
                pltpu.VMEM((SLOTS, BLOCKS, CHUNKS, LANES), F32),
                pltpu.VMEM((NEAR, 2, 8, CHUNKS, LANES), BF16),
                pltpu.VMEM((NEAR, 2, 2 * BLOCKS * CHUNKS, 4 * LANES), BF16),
                pltpu.SMEM((NEAR, BLOCKS), jnp.int32),
                pltpu.VMEM((BLOCKS, CHUNKS, LANES), F32),
                pltpu.VMEM((NEAR, 2, 2, FINE, LANES), F32),
                pltpu.VMEM((NEAR, 2, 4 * LANES, 2 * LANES), BF16),
                pltpu.VMEM((NEAR, 2, BLOCKS * CHUNKS, LANES), F32),
                pltpu.VMEM((BLOCKS * CHUNKS, LANES), F32),
                pltpu.VMEM((2, BLOCKS * FINE, NEAR * LANES), BF16),
                pltpu.VMEM((2, NEAR * LANES, BLOCKS * FINE), BF16),
                pltpu.VMEM((NEAR, NEAR, LANES, LANES), F32),
                pltpu.VMEM((NEAR, NEAR, LANES, LANES), F32),
                pltpu.VMEM((NEAR - 1, FINE + 8, LANES), F32),
                pltpu.VMEM((NEAR - 1, FINE + 8, LANES), F32),
                dma((2,)),
                dma,
                dma((3,)),
                dma((NEAR - 1,)),
                dma((NEAR - 1, 2)),
                dma((NEAR - 1,)),
                dma((NEAR - 1,)),
                dma((NEAR - 1, 4)),
            ],
            compiler_params=pltpu.CompilerParams(
                collective_id=0, has_side_effects=True, vmem_limit_bytes=40 << 20
            ),
        )(
            in_hbm(jnp.transpose(stiffness_blocks, (1, 0, 2))),
            in_hbm(block_columns),
            in_hbm(block_counts),
            in_hbm(tentative_tiles),
            in_hbm(aggregate_of),
        )
        return result.reshape(2, FINE, OFFSETS * LANES)

    by_device = P(("row", "col"), None)
    by_device3 = P(("row", "col"), None, None)
    return jax.shard_map(
        body,
        mesh=mesh,
        in_specs=(by_device3, by_device, by_device, by_device, P()),
        out_specs=by_device3,
        check_vma=False,
    )
```

```python
import jax
import jax.numpy as jnp
from jax import lax
from jax.experimental import pallas as pl
from jax.experimental.pallas import tpu as pltpu
from jax.sharding import PartitionSpec as P

MESH = pl.DeviceIdType.MESH
F32 = jnp.float32
BF16 = jnp.bfloat16

FINE = 64
BLOCKS = 8
SLOTS = 20
ROW_SLOTS = 4
CHUNKS = 32
LANES = 128
OMEGA = 2.0 / 3.0

ROW_STEPS = (0, 1, -1, 0, 0)
COL_STEPS = (0, 0, 0, -1, 1)
OPPOSITE = (0, 1, 2, 4, 3)
OFFSETS = 13
NEAR = 5
X_CHIPS = 4


def dot(a, b):
    return jnp.dot(a, b, preferred_element_type=F32)


def split(x):
    high = x.astype(BF16)
    return high, (x - high.astype(F32)).astype(BF16)


def kernel(
    rows,
    cols,
    stiff,
    columns_in,
    counts_in,
    tiles,
    aggs_in,
    out,
    columns,
    counts,
    aggs,
    xbuf,
    compact,
    dense,
    order,
    tp,
    tpack,
    weights,
    halves,
    damp,
    right,
    left,
    gsend,
    grecv,
    psend,
    precv,
    xsem,
    tsem,
    ssem,
    tsend,
    trecv,
    gsend_sem,
    psend_sem,
    grecv_sem,
):
    my_row = lax.axis_index("row")
    my_col = lax.axis_index("col")
    even = lax.rem(my_row, 2) == 0
    sign = jnp.where(even, 1, -1)
    places = [(my_row + sign * ROW_STEPS[q], my_col + COL_STEPS[q]) for q in range(NEAR)]
    exists = [
        True,
        True,
        (places[2][0] >= 0) & (places[2][0] < rows),
        my_col > 0,
        my_col < cols - 1,
    ]
    first_slots = [
        0,
        jnp.where(even, 16, 12),
        jnp.where(even, 12, 16),
        4,
        8,
    ]

    def band(row_units, col_step):
        if row_units == 0:
            return 6 + col_step
        ahead, behind = {1: (10, 2), -1: (2, 10), 2: (12, 0), -2: (0, 12)}[row_units]
        return jnp.where(even, ahead, behind) + col_step

    def band_of(q, m):
        turn = -1 if q in (1, 2) else 1
        return band(ROW_STEPS[q] + turn * ROW_STEPS[m], COL_STEPS[q] + COL_STEPS[m])

    def lanes_of(o):
        if isinstance(o, int):
            return slice(o * LANES, (o + 1) * LANES)
        return pl.ds(pl.multiple_of(o * LANES, LANES), LANES)

    def when_there(q):
        def run(f):
            if exists[q] is True:
                f()
            else:
                pl.when(exists[q])(f)

        return run

    left_far = lax.rem(my_col, X_CHIPS) == 0

    barrier = pltpu.get_barrier_semaphore()
    near_count = jnp.int32(1)
    for q in range(1, NEAR):
        if q > 1:
            near_count = near_count + jnp.where(exists[q], 1, 0)

        @when_there(q)
        def _():
            pl.semaphore_signal(barrier, inc=1, device_id=places[q], device_id_type=MESH)

    for i in range(CHUNKS):
        pltpu.make_async_copy(tiles.at[:, pl.ds(i * LANES, LANES)], tp.at[:, i, :], tsem).start()
    small = [
        pltpu.make_async_copy(columns_in, columns, ssem.at[0]),
        pltpu.make_async_copy(counts_in, counts, ssem.at[1]),
        pltpu.make_async_copy(aggs_in, aggs, ssem.at[2]),
    ]
    for copy in small:
        copy.start()
    for first, last, sem in ((0, ROW_SLOTS, xsem.at[0]), (ROW_SLOTS, SLOTS, xsem.at[1])):
        for i in range(CHUNKS):
            pltpu.make_async_copy(
                stiff.at[first:last, :, pl.ds(i * LANES, LANES)], xbuf.at[first:last, :, i, :], sem
            ).start()

    lane = lax.broadcasted_iota(jnp.int32, (1, LANES), 1)
    low_half = lane < FINE

    for copy in small:
        copy.wait()
    own_groups = None
    for q in range(NEAR):
        near_row = jnp.clip(places[q][0], 0, rows - 1)
        near_col = jnp.clip(places[q][1], 0, cols - 1)
        first = (near_row * cols + near_col) * BLOCKS
        groups = [aggs[first + j] & 1 for j in range(BLOCKS)]
        word = jnp.int32(0)
        ones = jnp.int32(0)
        for j in range(BLOCKS):
            at = jnp.where(groups[j] == 1, 4 + ones, j - ones)
            word = word | (jnp.int32(j) << (4 * at))
            ones = ones + groups[j]
        if q == 0:
            own_groups = groups
        for n in range(BLOCKS):
            order[q, n] = (word >> (4 * n)) & 7

    pltpu.make_async_copy(tp, tp, tsem).wait()
    for group in range(2):
        for pair in range(2):
            a = tp[order[0, 4 * group + 2 * pair]]
            b = tp[order[0, 4 * group + 2 * pair + 1]]
            tpack[0, group, pair, pl.ds(0, CHUNKS, 2), :] = jnp.where(low_half, a, pltpu.roll(b, FINE, 1))
            tpack[0, group, pair, pl.ds(1, CHUNKS, 2), :] = jnp.where(low_half, pltpu.roll(a, FINE, 1), b)

    def tile_copy(q, group):
        return pltpu.make_async_remote_copy(
            src_ref=tpack.at[0, group],
            dst_ref=tpack.at[OPPOSITE[q], group],
            send_sem=tsend.at[q - 1],
            recv_sem=trecv.at[OPPOSITE[q] - 1, group],
            device_id=places[q],
            device_id_type=MESH,
        )

    def arrival(q, group):
        return pltpu.make_async_remote_copy(
            src_ref=tpack.at[0, group],
            dst_ref=tpack.at[q, group],
            send_sem=tsend.at[q - 1],
            recv_sem=trecv.at[q - 1, group],
            device_id=places[q],
            device_id_type=MESH,
        )

    row_at = lax.broadcasted_iota(jnp.int32, (CHUNKS, LANES), 0)
    lane_at = lax.broadcasted_iota(jnp.int32, (CHUNKS, LANES), 1)

    zero = jnp.zeros((CHUNKS, LANES), BF16)
    for q in range(NEAR):
        compact[q, 0, 0] = zero
        compact[q, 1, 0] = zero

    def spread(q, k):
        slots = first_slots[q]
        rows_k = pl.ds(pl.multiple_of(k * CHUNKS, CHUNKS), CHUNKS)
        rows_low = pl.ds(pl.multiple_of(k * CHUNKS + 256, CHUNKS), CHUNKS)
        count = counts[k, slots // ROW_SLOTS]
        word = jnp.int32(0)
        for t in range(ROW_SLOTS):
            high, low = split(xbuf[slots + t, k])
            compact[q, 0, t + 1] = high
            compact[q, 1, t + 1] = low
            word = word | jnp.where(t < count, (t + 1) << (columns[k, slots + t] * 4), 0)
        for group in range(2):
            for n in range(4):
                e = (word >> (4 * order[q, 4 * group + n])) & 7
                lanes_n = slice(n * LANES, (n + 1) * LANES)
                dense[q, group, rows_k, lanes_n] = compact[q, 0, e]
                dense[q, group, rows_low, lanes_n] = compact[q, 1, e]

    def spread_own(k, _):
        x0 = xbuf[0, k]
        diagonal = [
            jnp.sum(
                jnp.where(lane_at == 2 * row_at + p * (FINE + 1), x0, 0.0), axis=1, keepdims=True
            )
            for p in range(2)
        ]
        rows_k = pl.ds(pl.multiple_of(k * CHUNKS, CHUNKS), CHUNKS)
        damp[rows_k, :] = OMEGA / jnp.where(low_half, diagonal[0], diagonal[1])
        spread(0, k)
        return 0

    def spread_near(k, _):
        for q in range(1, NEAR):
            spread(q, k)
        return 0

    def smooth_half(q, group):
        for pair in range(2):
            v = tpack[q, group, pair]
            r = pltpu.roll(v, FINE, 1)
            for part, (v_part, r_part) in enumerate(zip(split(v), split(r))):
                lanes_part = slice(part * LANES, (part + 1) * LANES)
                none = jnp.zeros_like(v_part)
                tiles_at = (
                    jnp.where(low_half, v_part, none),
                    jnp.where(low_half, none, r_part),
                    jnp.where(low_half, r_part, none),
                    jnp.where(low_half, none, v_part),
                )
                for n in range(4):
                    rows_n = slice((4 * pair + n) * FINE, (4 * pair + n + 1) * FINE)
                    weights[q, group, rows_n, lanes_part] = tiles_at[n]
        x = dot(dense[q, group, :256], weights[q, group])
        y = dot(dense[q, group, 256:], weights[q, group, :, :LANES])
        s = x[:, :LANES] + (x[:, LANES:] + y)
        halves[q, group] = s
        l = -(damp[...] * s)
        if q == 0:
            own = [jnp.where(own_groups[k] == group, tp[k], 0.0) for k in range(BLOCKS)]
            l = l + jnp.concatenate(own, axis=0)
        first = q * LANES + group * FINE
        for part, l_part in enumerate(split(l.T)):
            for p in range(2):
                left[part, first : first + FINE, p * 256 : (p + 1) * 256] = l_part[p * FINE : (p + 1) * FINE]

    def make_right(q):
        s_0, s_1 = halves[q, 0], halves[q, 1]
        by_parity = (
            jnp.where(low_half, s_0, pltpu.roll(s_1, FINE, 1)),
            jnp.where(low_half, pltpu.roll(s_0, FINE, 1), s_1),
        )
        for p in range(2):
            for part, r_part in enumerate(split(by_parity[p])):
                right[part, p * 256 : (p + 1) * 256, lanes_of(q)] = r_part

    def smooth(q):
        smooth_half(q, 0)
        smooth_half(q, 1)
        make_right(q)

    def products(row_list, m_from, m_to):
        cols_r = slice(m_from * LANES, m_to * LANES)
        highs = jnp.concatenate([left[0, a : a + n, :] for a, n in row_list], axis=0)
        lows = jnp.concatenate([left[1, a : a + n, :] for a, n in row_list], axis=0)
        return (
            dot(highs, right[0, :, cols_r])
            + dot(lows, right[0, :, cols_r])
            + dot(highs, right[1, :, cols_r])
        )

    square_row = lax.broadcasted_iota(jnp.int32, (FINE, FINE), 0)
    square_col = lax.broadcasted_iota(jnp.int32, (FINE, FINE), 1)

    def packed(g):
        a, b, c = g[:FINE, :FINE], g[:FINE, FINE:], g[FINE:, FINE:]
        square = jnp.where(square_row >= square_col, a, c)
        diagonal = jnp.sum(jnp.where(square_row == square_col, c, 0.0), axis=0, keepdims=True)
        top = jnp.concatenate([square, b], axis=1)
        last = jnp.broadcast_to(jnp.concatenate([diagonal, diagonal], axis=1), (8, LANES))
        return jnp.concatenate([top, last], axis=0)

    def unpacked(x):
        square, b = x[:FINE, :FINE], x[:FINE, FINE:]
        diagonal = x[FINE : FINE + 1, :FINE]
        turned = x[:FINE].T
        square_t, b_t = turned[:FINE], turned[FINE:]
        a = jnp.where(square_row >= square_col, square, square_t)
        c = jnp.where(square_row < square_col, square, square_t)
        c = jnp.where(square_row == square_col, diagonal, c)
        return jnp.concatenate(
            [jnp.concatenate([a, b], axis=1), jnp.concatenate([b_t, c], axis=1)], axis=0
        )

    def piece_copy(q, m, group):
        to = OPPOSITE[q]
        recv_sem = grecv_sem.at[to - 1, max(m - 1, 0)]
        if m == q and q > 1:
            return pltpu.make_async_remote_copy(
                src_ref=psend.at[q - 1],
                dst_ref=precv.at[to - 1],
                send_sem=psend_sem.at[q - 1],
                recv_sem=recv_sem,
                device_id=places[q],
                device_id_type=MESH,
            )
        at = pl.ds(0, LANES) if group is None else pl.ds(group * FINE, FINE)
        return pltpu.make_async_remote_copy(
            src_ref=gsend.at[q, m, at],
            dst_ref=grecv.at[to, m, at],
            send_sem=gsend_sem.at[q - 1],
            recv_sem=recv_sem,
            device_id=places[q],
            device_id_type=MESH,
        )

    def set_arrival(q, m_from, m_to):
        alone = m_from == OPPOSITE[q] and q > 1
        return pltpu.make_async_remote_copy(
            src_ref=psend.at[q - 1] if alone else gsend.at[q, m_from:m_to],
            dst_ref=precv.at[q - 1] if alone else grecv.at[q, m_from:m_to],
            send_sem=gsend_sem.at[q - 1],
            recv_sem=grecv_sem.at[q - 1, max(m_from - 1, 0)],
            device_id=places[q],
            device_id_type=MESH,
        )

    def all_sent(q):
        pltpu.make_async_remote_copy(
            src_ref=tpack.at[0],
            dst_ref=tpack.at[OPPOSITE[q]],
            send_sem=tsend.at[q - 1],
            recv_sem=trecv.at[q - 1, 0],
            device_id=places[q],
            device_id_type=MESH,
        ).wait_send()
        pltpu.make_async_remote_copy(
            src_ref=gsend.at[q, 0:4] if q > 1 else gsend.at[q],
            dst_ref=grecv.at[q, 0:4] if q > 1 else grecv.at[q],
            send_sem=gsend_sem.at[q - 1],
            recv_sem=grecv_sem.at[q - 1, 0],
            device_id=places[q],
            device_id_type=MESH,
        ).wait_send()
        if q > 1:
            piece_copy(q, q, None).wait_send()

    def start_pieces(q, m_from, m_to, group):
        @when_there(q)
        def _():
            for m in sorted(range(m_from, m_to), key=lambda m: m != q):
                piece_copy(q, m, group).start()

    def make_and_send(q_list, m_from, m_to):
        g = products([(q * LANES, LANES) for q in q_list], m_from, m_to)
        for at, q in enumerate(q_list):
            for m in range(m_from, m_to):
                part = g[at * LANES : (at + 1) * LANES, (m - m_from) * LANES : (m - m_from + 1) * LANES]
                if q == 0:
                    out[:, lanes_of(band_of(0, m))] = part
                elif m == q and q > 1:
                    psend[q - 1] = packed(part)
                else:
                    gsend[q, m] = part
        if q_list == (3, 4):
            far_first(lambda q: start_pieces(q, m_from, m_to, None))
        else:
            for q in q_list:
                if q > 0:
                    start_pieces(q, m_from, m_to, None)

    def make_and_send_halves(group, m_from, m_to):
        g = products([(q * LANES + group * FINE, FINE) for q in (3, 4)], m_from, m_to)
        for at, q in enumerate((3, 4)):
            for m in range(m_from, m_to):
                gsend[q, m, group * FINE : (group + 1) * FINE] = g[
                    at * FINE : (at + 1) * FINE, (m - m_from) * LANES : (m - m_from + 1) * LANES
                ]
        far_first(lambda q: start_pieces(q, m_from, m_to, group))

    def wait_tiles(q, group):
        @when_there(q)
        def _():
            arrival(q, group).wait_recv()

    pl.semaphore_wait(barrier, near_count)
    def send_tiles(q, group):
        @when_there(q)
        def _():
            tile_copy(q, group).start()

    def far_first(send):
        @pl.when(left_far)
        def _():
            send(3)
            send(4)

        @pl.when(jnp.logical_not(left_far))
        def _():
            send(4)
            send(3)

    for group in range(2):
        far_first(lambda q: send_tiles(q, group))
        for q in (2, 1):
            send_tiles(q, group)

    for q in range(2, NEAR):

        @pl.when(jnp.logical_not(exists[q]))
        def _():
            tpack[q] = jnp.zeros((2, 2, FINE, LANES), F32)

    for o in range(OFFSETS):
        if o not in (2, 5, 6, 7, 10):
            out[:, lanes_of(o)] = jnp.zeros((LANES, LANES), F32)

    pltpu.make_async_copy(xbuf.at[0:ROW_SLOTS], xbuf.at[0:ROW_SLOTS], xsem.at[0]).wait()
    lax.fori_loop(0, BLOCKS, spread_own, 0)
    pltpu.make_async_copy(xbuf.at[ROW_SLOTS:SLOTS], xbuf.at[ROW_SLOTS:SLOTS], xsem.at[1]).wait()
    lax.fori_loop(0, BLOCKS, spread_near, 0)
    smooth(0)
    wait_tiles(1, 0)
    wait_tiles(1, 1)
    smooth(1)
    make_and_send((1,), 0, 2)
    make_and_send((0,), 0, 2)
    for group in range(2):
        wait_tiles(3, group)
        wait_tiles(4, group)
        smooth_half(3, group)
        smooth_half(4, group)
        make_and_send_halves(group, 0, 2)
    wait_tiles(2, 0)
    wait_tiles(2, 1)
    smooth(2)
    make_and_send((2,), 0, 2)
    make_right(3)
    make_right(4)
    make_and_send((3, 4), 2, 5)
    make_and_send((2,), 2, 5)
    make_and_send((1,), 2, 5)
    make_and_send((0,), 2, 5)

    for q_list, m_from, m_to in (
        ((1,), 0, 2),
        ((3, 4), 0, 2),
        ((1,), 2, 3),
        ((1,), 3, 4),
        ((1,), 4, 5),
        ((2,), 0, 2),
        ((3, 4), 2, 3),
        ((2,), 2, 3),
        ((2,), 3, 4),
        ((2,), 4, 5),
        ((4,), 3, 4),
        ((3,), 4, 5),
        ((3,), 3, 4),
        ((4,), 4, 5),
    ):
        for q in q_list:

            @when_there(q)
            def _():
                set_arrival(q, m_from, m_to).wait_recv()
                for m in range(m_from, m_to):
                    o = lanes_of(band_of(q, m))
                    if q > 1 and m == OPPOSITE[q]:
                        out[:, o] += unpacked(precv[q - 1])
                    else:
                        out[:, o] += grecv[q, m]

    for q in range(1, NEAR):

        @when_there(q)
        def _():
            all_sent(q)


def solution(mesh):
    rows, cols = mesh.shape["row"], mesh.shape["col"]

    def body(stiffness_blocks, block_columns, block_counts, tentative_tiles, aggregate_of):
        any_spec = pl.BlockSpec(memory_space=pl.ANY)
        in_hbm = lambda x: pltpu.with_memory_space_constraint(x, pltpu.HBM)
        dma = pltpu.SemaphoreType.DMA
        result = pl.pallas_call(
            lambda *refs: kernel(rows, cols, *refs),
            out_shape=jax.ShapeDtypeStruct((2 * FINE, OFFSETS * LANES), F32),
            in_specs=[any_spec] * 5,
            out_specs=pl.BlockSpec(memory_space=pltpu.VMEM),
            scratch_shapes=[
                pltpu.SMEM((BLOCKS, SLOTS), jnp.int32),
                pltpu.SMEM((BLOCKS, NEAR), jnp.int32),
                pltpu.SMEM(aggregate_of.shape, jnp.int32),
                pltpu.VMEM((SLOTS, BLOCKS, CHUNKS, LANES), F32),
                pltpu.VMEM((NEAR, 2, 8, CHUNKS, LANES), BF16),
                pltpu.VMEM((NEAR, 2, 2 * BLOCKS * CHUNKS, 4 * LANES), BF16),
                pltpu.SMEM((NEAR, BLOCKS), jnp.int32),
                pltpu.VMEM((BLOCKS, CHUNKS, LANES), F32),
                pltpu.VMEM((NEAR, 2, 2, FINE, LANES), F32),
                pltpu.VMEM((NEAR, 2, 4 * LANES, 2 * LANES), BF16),
                pltpu.VMEM((NEAR, 2, BLOCKS * CHUNKS, LANES), F32),
                pltpu.VMEM((BLOCKS * CHUNKS, LANES), F32),
                pltpu.VMEM((2, BLOCKS * FINE, NEAR * LANES), BF16),
                pltpu.VMEM((2, NEAR * LANES, BLOCKS * FINE), BF16),
                pltpu.VMEM((NEAR, NEAR, LANES, LANES), F32),
                pltpu.VMEM((NEAR, NEAR, LANES, LANES), F32),
                pltpu.VMEM((NEAR - 1, FINE + 8, LANES), F32),
                pltpu.VMEM((NEAR - 1, FINE + 8, LANES), F32),
                dma((2,)),
                dma,
                dma((3,)),
                dma((NEAR - 1,)),
                dma((NEAR - 1, 2)),
                dma((NEAR - 1,)),
                dma((NEAR - 1,)),
                dma((NEAR - 1, 4)),
            ],
            compiler_params=pltpu.CompilerParams(
                collective_id=0, has_side_effects=True, vmem_limit_bytes=40 << 20
            ),
        )(
            in_hbm(jnp.transpose(stiffness_blocks, (1, 0, 2))),
            in_hbm(block_columns),
            in_hbm(block_counts),
            in_hbm(tentative_tiles),
            in_hbm(aggregate_of),
        )
        return result.reshape(2, FINE, OFFSETS * LANES)

    by_device = P(("row", "col"), None)
    by_device3 = P(("row", "col"), None, None)
    return jax.shard_map(
        body,
        mesh=mesh,
        in_specs=(by_device3, by_device, by_device, by_device, P()),
        out_specs=by_device3,
        check_vma=False,
    )
```

```python
import jax
import jax.numpy as jnp
from jax import lax
from jax.experimental import pallas as pl
from jax.experimental.pallas import tpu as pltpu
from jax.sharding import PartitionSpec as P

MESH = pl.DeviceIdType.MESH
F32 = jnp.float32
BF16 = jnp.bfloat16

FINE = 64
BLOCKS = 8
SLOTS = 20
ROW_SLOTS = 4
CHUNKS = 32
LANES = 128
OMEGA = 2.0 / 3.0

ROW_STEPS = (0, 1, -1, 0, 0)
COL_STEPS = (0, 0, 0, -1, 1)
OPPOSITE = (0, 1, 2, 4, 3)
OFFSETS = 13
NEAR = 5
X_CHIPS = 4


def dot(a, b):
    return jnp.dot(a, b, preferred_element_type=F32)


def split(x):
    high = x.astype(BF16)
    return high, (x - high.astype(F32)).astype(BF16)


def kernel(
    rows,
    cols,
    stiff,
    columns_in,
    counts_in,
    tiles,
    aggs_in,
    out,
    columns,
    counts,
    aggs,
    xbuf,
    compact,
    dense,
    order,
    tp,
    tpack,
    weights,
    halves,
    damp,
    right,
    left,
    gsend,
    grecv,
    psend,
    precv,
    xsem,
    tsem,
    ssem,
    tsend,
    trecv,
    gsend_sem,
    psend_sem,
    grecv_sem,
):
    my_row = lax.axis_index("row")
    my_col = lax.axis_index("col")
    even = lax.rem(my_row, 2) == 0
    sign = jnp.where(even, 1, -1)
    places = [(my_row + sign * ROW_STEPS[q], my_col + COL_STEPS[q]) for q in range(NEAR)]
    exists = [
        True,
        True,
        (places[2][0] >= 0) & (places[2][0] < rows),
        my_col > 0,
        my_col < cols - 1,
    ]
    first_slots = [
        0,
        jnp.where(even, 16, 12),
        jnp.where(even, 12, 16),
        4,
        8,
    ]

    def band(row_units, col_step):
        if row_units == 0:
            return 6 + col_step
        ahead, behind = {1: (10, 2), -1: (2, 10), 2: (12, 0), -2: (0, 12)}[row_units]
        return jnp.where(even, ahead, behind) + col_step

    def band_of(q, m):
        turn = -1 if q in (1, 2) else 1
        return band(ROW_STEPS[q] + turn * ROW_STEPS[m], COL_STEPS[q] + COL_STEPS[m])

    def lanes_of(o):
        if isinstance(o, int):
            return slice(o * LANES, (o + 1) * LANES)
        return pl.ds(pl.multiple_of(o * LANES, LANES), LANES)

    def when_there(q):
        def run(f):
            if exists[q] is True:
                f()
            else:
                pl.when(exists[q])(f)

        return run

    left_far = lax.rem(my_col, X_CHIPS) == 0

    barrier = pltpu.get_barrier_semaphore()
    near_count = jnp.int32(1)
    for q in range(1, NEAR):
        if q > 1:
            near_count = near_count + jnp.where(exists[q], 1, 0)

        @when_there(q)
        def _():
            pl.semaphore_signal(barrier, inc=1, device_id=places[q], device_id_type=MESH)

    for i in range(CHUNKS):
        pltpu.make_async_copy(tiles.at[:, pl.ds(i * LANES, LANES)], tp.at[:, i, :], tsem).start()
    small = [
        pltpu.make_async_copy(columns_in, columns, ssem.at[0]),
        pltpu.make_async_copy(counts_in, counts, ssem.at[1]),
        pltpu.make_async_copy(aggs_in, aggs, ssem.at[2]),
    ]
    for copy in small:
        copy.start()
    for first, last, sem in ((0, ROW_SLOTS, xsem.at[0]), (ROW_SLOTS, SLOTS, xsem.at[1])):
        for i in range(CHUNKS):
            pltpu.make_async_copy(
                stiff.at[first:last, :, pl.ds(i * LANES, LANES)], xbuf.at[first:last, :, i, :], sem
            ).start()

    lane = lax.broadcasted_iota(jnp.int32, (1, LANES), 1)
    low_half = lane < FINE

    for copy in small:
        copy.wait()
    own_groups = None
    for q in range(NEAR):
        near_row = jnp.clip(places[q][0], 0, rows - 1)
        near_col = jnp.clip(places[q][1], 0, cols - 1)
        first = (near_row * cols + near_col) * BLOCKS
        groups = [aggs[first + j] & 1 for j in range(BLOCKS)]
        word = jnp.int32(0)
        ones = jnp.int32(0)
        for j in range(BLOCKS):
            at = jnp.where(groups[j] == 1, 4 + ones, j - ones)
            word = word | (jnp.int32(j) << (4 * at))
            ones = ones + groups[j]
        if q == 0:
            own_groups = groups
        for n in range(BLOCKS):
            order[q, n] = (word >> (4 * n)) & 7

    pltpu.make_async_copy(tp, tp, tsem).wait()
    for group in range(2):
        for pair in range(2):
            a = tp[order[0, 4 * group + 2 * pair]]
            b = tp[order[0, 4 * group + 2 * pair + 1]]
            tpack[0, group, pair, pl.ds(0, CHUNKS, 2), :] = jnp.where(low_half, a, pltpu.roll(b, FINE, 1))
            tpack[0, group, pair, pl.ds(1, CHUNKS, 2), :] = jnp.where(low_half, pltpu.roll(a, FINE, 1), b)

    def tile_sem(q, group):
        return 2 * (q - 2) + group if q > 2 else q - 1

    def tile_copy(q, group):
        return pltpu.make_async_remote_copy(
            src_ref=tpack.at[0, group],
            dst_ref=tpack.at[OPPOSITE[q], group],
            send_sem=tsend.at[q - 1],
            recv_sem=trecv.at[tile_sem(OPPOSITE[q], group)],
            device_id=places[q],
            device_id_type=MESH,
        )

    def arrival(q, group):
        return pltpu.make_async_remote_copy(
            src_ref=tpack.at[0, group] if q > 2 else tpack.at[0],
            dst_ref=tpack.at[q, group] if q > 2 else tpack.at[q],
            send_sem=tsend.at[q - 1],
            recv_sem=trecv.at[tile_sem(q, group)],
            device_id=places[q],
            device_id_type=MESH,
        )

    row_at = lax.broadcasted_iota(jnp.int32, (CHUNKS, LANES), 0)
    lane_at = lax.broadcasted_iota(jnp.int32, (CHUNKS, LANES), 1)

    zero = jnp.zeros((CHUNKS, LANES), BF16)
    for q in range(NEAR):
        compact[q, 0, 0] = zero
        compact[q, 1, 0] = zero

    def spread(q, k):
        slots = first_slots[q]
        rows_k = pl.ds(pl.multiple_of(k * CHUNKS, CHUNKS), CHUNKS)
        rows_low = pl.ds(pl.multiple_of(k * CHUNKS + 256, CHUNKS), CHUNKS)
        count = counts[k, slots // ROW_SLOTS]
        word = jnp.int32(0)
        for t in range(ROW_SLOTS):
            high, low = split(xbuf[slots + t, k])
            compact[q, 0, t + 1] = high
            compact[q, 1, t + 1] = low
            word = word | jnp.where(t < count, (t + 1) << (columns[k, slots + t] * 4), 0)
        for group in range(2):
            for n in range(4):
                e = (word >> (4 * order[q, 4 * group + n])) & 7
                lanes_n = slice(n * LANES, (n + 1) * LANES)
                dense[q, group, rows_k, lanes_n] = compact[q, 0, e]
                dense[q, group, rows_low, lanes_n] = compact[q, 1, e]

    def spread_own(k, _):
        x0 = xbuf[0, k]
        diagonal = [
            jnp.sum(
                jnp.where(lane_at == 2 * row_at + p * (FINE + 1), x0, 0.0), axis=1, keepdims=True
            )
            for p in range(2)
        ]
        rows_k = pl.ds(pl.multiple_of(k * CHUNKS, CHUNKS), CHUNKS)
        damp[rows_k, :] = OMEGA / jnp.where(low_half, diagonal[0], diagonal[1])
        spread(0, k)
        return 0

    def spread_near(k, _):
        for q in range(1, NEAR):
            spread(q, k)
        return 0

    def smooth_half(q, group):
        for pair in range(2):
            v = tpack[q, group, pair]
            r = pltpu.roll(v, FINE, 1)
            for part, (v_part, r_part) in enumerate(zip(split(v), split(r))):
                lanes_part = slice(part * LANES, (part + 1) * LANES)
                none = jnp.zeros_like(v_part)
                tiles_at = (
                    jnp.where(low_half, v_part, none),
                    jnp.where(low_half, none, r_part),
                    jnp.where(low_half, r_part, none),
                    jnp.where(low_half, none, v_part),
                )
                for n in range(4):
                    rows_n = slice((4 * pair + n) * FINE, (4 * pair + n + 1) * FINE)
                    weights[q, group, rows_n, lanes_part] = tiles_at[n]
        x = dot(dense[q, group, :256], weights[q, group])
        y = dot(dense[q, group, 256:], weights[q, group, :, :LANES])
        s = x[:, :LANES] + (x[:, LANES:] + y)
        halves[q, group] = s
        l = -(damp[...] * s)
        if q == 0:
            own = [jnp.where(own_groups[k] == group, tp[k], 0.0) for k in range(BLOCKS)]
            l = l + jnp.concatenate(own, axis=0)
        first = q * LANES + group * FINE
        for part, l_part in enumerate(split(l.T)):
            for p in range(2):
                left[part, first : first + FINE, p * 256 : (p + 1) * 256] = l_part[p * FINE : (p + 1) * FINE]

    def make_right(q):
        s_0, s_1 = halves[q, 0], halves[q, 1]
        by_parity = (
            jnp.where(low_half, s_0, pltpu.roll(s_1, FINE, 1)),
            jnp.where(low_half, pltpu.roll(s_0, FINE, 1), s_1),
        )
        for p in range(2):
            for part, r_part in enumerate(split(by_parity[p])):
                right[part, p * 256 : (p + 1) * 256, lanes_of(q)] = r_part

    def smooth(q):
        smooth_half(q, 0)
        smooth_half(q, 1)
        make_right(q)

    def products(row_list, m_from, m_to):
        cols_r = slice(m_from * LANES, m_to * LANES)
        highs = jnp.concatenate([left[0, a : a + n, :] for a, n in row_list], axis=0)
        lows = jnp.concatenate([left[1, a : a + n, :] for a, n in row_list], axis=0)
        return (
            dot(highs, right[0, :, cols_r])
            + dot(lows, right[0, :, cols_r])
            + dot(highs, right[1, :, cols_r])
        )

    square_row = lax.broadcasted_iota(jnp.int32, (FINE, FINE), 0)
    square_col = lax.broadcasted_iota(jnp.int32, (FINE, FINE), 1)

    def packed(g):
        a, b, c = g[:FINE, :FINE], g[:FINE, FINE:], g[FINE:, FINE:]
        square = jnp.where(square_row >= square_col, a, c)
        diagonal = jnp.sum(jnp.where(square_row == square_col, c, 0.0), axis=0, keepdims=True)
        top = jnp.concatenate([square, b], axis=1)
        last = jnp.broadcast_to(jnp.concatenate([diagonal, diagonal], axis=1), (8, LANES))
        return jnp.concatenate([top, last], axis=0)

    def unpacked(x):
        square, b = x[:FINE, :FINE], x[:FINE, FINE:]
        diagonal = x[FINE : FINE + 1, :FINE]
        turned = x[:FINE].T
        square_t, b_t = turned[:FINE], turned[FINE:]
        a = jnp.where(square_row >= square_col, square, square_t)
        c = jnp.where(square_row < square_col, square, square_t)
        c = jnp.where(square_row == square_col, diagonal, c)
        return jnp.concatenate(
            [jnp.concatenate([a, b], axis=1), jnp.concatenate([b_t, c], axis=1)], axis=0
        )

    def set_sem(q, m):
        return 0 if q == 1 else 1 + 4 * (q - 2) + max(m - 1, 0)

    def piece_copy(q, m, group):
        to = OPPOSITE[q]
        recv_sem = grecv_sem.at[set_sem(to, m)]
        if m == q and q > 1:
            return pltpu.make_async_remote_copy(
                src_ref=psend.at[q - 1],
                dst_ref=precv.at[to - 1],
                send_sem=psend_sem.at[q - 1],
                recv_sem=recv_sem,
                device_id=places[q],
                device_id_type=MESH,
            )
        at = pl.ds(0, LANES) if group is None else pl.ds(group * FINE, FINE)
        return pltpu.make_async_remote_copy(
            src_ref=gsend.at[q, m, at],
            dst_ref=grecv.at[to, m, at],
            send_sem=gsend_sem.at[q - 1],
            recv_sem=recv_sem,
            device_id=places[q],
            device_id_type=MESH,
        )

    def set_arrival(q, m_from, m_to):
        alone = m_from == OPPOSITE[q] and q > 1
        return pltpu.make_async_remote_copy(
            src_ref=psend.at[q - 1] if alone else gsend.at[q, m_from:m_to],
            dst_ref=precv.at[q - 1] if alone else grecv.at[q, m_from:m_to],
            send_sem=gsend_sem.at[q - 1],
            recv_sem=grecv_sem.at[set_sem(q, m_from)],
            device_id=places[q],
            device_id_type=MESH,
        )

    def all_sent(q):
        pltpu.make_async_remote_copy(
            src_ref=tpack.at[0],
            dst_ref=tpack.at[OPPOSITE[q]],
            send_sem=tsend.at[q - 1],
            recv_sem=trecv.at[tile_sem(q, 0)],
            device_id=places[q],
            device_id_type=MESH,
        ).wait_send()
        pltpu.make_async_remote_copy(
            src_ref=gsend.at[q, 0:4] if q > 1 else gsend.at[q],
            dst_ref=grecv.at[q, 0:4] if q > 1 else grecv.at[q],
            send_sem=gsend_sem.at[q - 1],
            recv_sem=grecv_sem.at[set_sem(q, 0)],
            device_id=places[q],
            device_id_type=MESH,
        ).wait_send()
        if q > 1:
            piece_copy(q, q, None).wait_send()

    def start_pieces(q, m_from, m_to, group):
        @when_there(q)
        def _():
            for m in sorted(range(m_from, m_to), key=lambda m: m != q):
                piece_copy(q, m, group).start()

    def make_and_send(q_list, m_from, m_to):
        g = products([(q * LANES, LANES) for q in q_list], m_from, m_to)
        for at, q in enumerate(q_list):
            for m in range(m_from, m_to):
                part = g[at * LANES : (at + 1) * LANES, (m - m_from) * LANES : (m - m_from + 1) * LANES]
                if q == 0:
                    out[:, lanes_of(band_of(0, m))] = part
                elif m == q and q > 1:
                    psend[q - 1] = packed(part)
                else:
                    gsend[q, m] = part
        if q_list == (3, 4):
            far_first(lambda q: start_pieces(q, m_from, m_to, None))
        else:
            for q in q_list:
                if q > 0:
                    start_pieces(q, m_from, m_to, None)

    def make_and_send_halves(group, m_from, m_to):
        g = products([(q * LANES + group * FINE, FINE) for q in (3, 4)], m_from, m_to)
        for at, q in enumerate((3, 4)):
            for m in range(m_from, m_to):
                gsend[q, m, group * FINE : (group + 1) * FINE] = g[
                    at * FINE : (at + 1) * FINE, (m - m_from) * LANES : (m - m_from + 1) * LANES
                ]
        far_first(lambda q: start_pieces(q, m_from, m_to, group))

    def wait_tiles(q, group):
        @when_there(q)
        def _():
            arrival(q, group).wait_recv()

    pl.semaphore_wait(barrier, near_count)
    def send_tiles(q, group):
        @when_there(q)
        def _():
            tile_copy(q, group).start()

    def far_first(send):
        @pl.when(left_far)
        def _():
            send(3)
            send(4)

        @pl.when(jnp.logical_not(left_far))
        def _():
            send(4)
            send(3)

    for group in range(2):
        far_first(lambda q: send_tiles(q, group))
        for q in (2, 1):
            send_tiles(q, group)

    for q in range(2, NEAR):

        @pl.when(jnp.logical_not(exists[q]))
        def _():
            tpack[q] = jnp.zeros((2, 2, FINE, LANES), F32)

    for o in range(OFFSETS):
        if o not in (2, 5, 6, 7, 10):
            out[:, lanes_of(o)] = jnp.zeros((LANES, LANES), F32)

    pltpu.make_async_copy(xbuf.at[0:ROW_SLOTS], xbuf.at[0:ROW_SLOTS], xsem.at[0]).wait()
    lax.fori_loop(0, BLOCKS, spread_own, 0)
    pltpu.make_async_copy(xbuf.at[ROW_SLOTS:SLOTS], xbuf.at[ROW_SLOTS:SLOTS], xsem.at[1]).wait()
    lax.fori_loop(0, BLOCKS, spread_near, 0)
    smooth(0)
    wait_tiles(1, 0)
    smooth(1)
    make_and_send((0, 1), 0, 2)
    for group in range(2):
        wait_tiles(3, group)
        wait_tiles(4, group)
        smooth_half(3, group)
        smooth_half(4, group)
        make_and_send_halves(group, 0, 2)
    wait_tiles(2, 0)
    smooth(2)
    make_and_send((2,), 0, 2)
    make_right(3)
    make_right(4)
    make_and_send((3, 4), 2, 5)
    make_and_send((2,), 2, 5)
    make_and_send((0, 1), 2, 5)

    for q_list, m_from, m_to in (
        ((3, 4), 0, 2),
        ((2,), 0, 2),
        ((1,), 0, 5),
        ((3, 4), 2, 3),
        ((2,), 2, 3),
        ((2,), 3, 4),
        ((2,), 4, 5),
        ((4,), 3, 4),
        ((3,), 4, 5),
        ((3,), 3, 4),
        ((4,), 4, 5),
    ):
        for q in q_list:

            @when_there(q)
            def _():
                set_arrival(q, m_from, m_to).wait_recv()
                for m in range(m_from, m_to):
                    o = lanes_of(band_of(q, m))
                    if q > 1 and m == OPPOSITE[q]:
                        out[:, o] += unpacked(precv[q - 1])
                    else:
                        out[:, o] += grecv[q, m]

    for q in range(1, NEAR):

        @when_there(q)
        def _():
            all_sent(q)


def solution(mesh):
    rows, cols = mesh.shape["row"], mesh.shape["col"]

    def body(stiffness_blocks, block_columns, block_counts, tentative_tiles, aggregate_of):
        any_spec = pl.BlockSpec(memory_space=pl.ANY)
        in_hbm = lambda x: pltpu.with_memory_space_constraint(x, pltpu.HBM)
        dma = pltpu.SemaphoreType.DMA
        result = pl.pallas_call(
            lambda *refs: kernel(rows, cols, *refs),
            out_shape=jax.ShapeDtypeStruct((2 * FINE, OFFSETS * LANES), F32),
            in_specs=[any_spec] * 5,
            out_specs=pl.BlockSpec(memory_space=pltpu.VMEM),
            scratch_shapes=[
                pltpu.SMEM((BLOCKS, SLOTS), jnp.int32),
                pltpu.SMEM((BLOCKS, NEAR), jnp.int32),
                pltpu.SMEM(aggregate_of.shape, jnp.int32),
                pltpu.VMEM((SLOTS, BLOCKS, CHUNKS, LANES), F32),
                pltpu.VMEM((NEAR, 2, 8, CHUNKS, LANES), BF16),
                pltpu.VMEM((NEAR, 2, 2 * BLOCKS * CHUNKS, 4 * LANES), BF16),
                pltpu.SMEM((NEAR, BLOCKS), jnp.int32),
                pltpu.VMEM((BLOCKS, CHUNKS, LANES), F32),
                pltpu.VMEM((NEAR, 2, 2, FINE, LANES), F32),
                pltpu.VMEM((NEAR, 2, 4 * LANES, 2 * LANES), BF16),
                pltpu.VMEM((NEAR, 2, BLOCKS * CHUNKS, LANES), F32),
                pltpu.VMEM((BLOCKS * CHUNKS, LANES), F32),
                pltpu.VMEM((2, BLOCKS * FINE, NEAR * LANES), BF16),
                pltpu.VMEM((2, NEAR * LANES, BLOCKS * FINE), BF16),
                pltpu.VMEM((NEAR, NEAR, LANES, LANES), F32),
                pltpu.VMEM((NEAR, NEAR, LANES, LANES), F32),
                pltpu.VMEM((NEAR - 1, FINE + 8, LANES), F32),
                pltpu.VMEM((NEAR - 1, FINE + 8, LANES), F32),
                dma((2,)),
                dma,
                dma((3,)),
                dma((NEAR - 1,)),
                dma((6,)),
                dma((NEAR - 1,)),
                dma((NEAR - 1,)),
                dma((13,)),
            ],
            compiler_params=pltpu.CompilerParams(
                collective_id=0, has_side_effects=True, vmem_limit_bytes=40 << 20
            ),
        )(
            in_hbm(jnp.transpose(stiffness_blocks, (1, 0, 2))),
            in_hbm(block_columns),
            in_hbm(block_counts),
            in_hbm(tentative_tiles),
            in_hbm(aggregate_of),
        )
        return result.reshape(2, FINE, OFFSETS * LANES)

    by_device = P(("row", "col"), None)
    by_device3 = P(("row", "col"), None, None)
    return jax.shard_map(
        body,
        mesh=mesh,
        in_specs=(by_device3, by_device, by_device, by_device, P()),
        out_specs=by_device3,
        check_vma=False,
    )
```

```python
import jax
import jax.numpy as jnp
from jax import lax
from jax.experimental import pallas as pl
from jax.experimental.pallas import tpu as pltpu
from jax.sharding import PartitionSpec as P

MESH = pl.DeviceIdType.MESH
F32 = jnp.float32
BF16 = jnp.bfloat16

FINE = 64
BLOCKS = 8
SLOTS = 20
ROW_SLOTS = 4
CHUNKS = 32
LANES = 128
OMEGA = 2.0 / 3.0

ROW_STEPS = (0, 1, -1, 0, 0)
COL_STEPS = (0, 0, 0, -1, 1)
OPPOSITE = (0, 1, 2, 4, 3)
OFFSETS = 13
NEAR = 5
X_CHIPS = 4


def dot(a, b):
    return jnp.dot(a, b, preferred_element_type=F32)


def split(x):
    high = x.astype(BF16)
    return high, (x - high.astype(F32)).astype(BF16)


def kernel(
    rows,
    cols,
    stiff,
    columns_in,
    counts_in,
    tiles,
    aggs_in,
    out,
    columns,
    counts,
    aggs,
    xbuf,
    compact,
    dense,
    order,
    tp,
    tpack,
    weights,
    halves,
    damp,
    right,
    left,
    gsend,
    grecv,
    psend,
    precv,
    xsem,
    tsem,
    ssem,
    tsend,
    trecv,
    gsend_sem,
    psend_sem,
    grecv_sem,
):
    my_row = lax.axis_index("row")
    my_col = lax.axis_index("col")
    even = lax.rem(my_row, 2) == 0
    sign = jnp.where(even, 1, -1)
    places = [(my_row + sign * ROW_STEPS[q], my_col + COL_STEPS[q]) for q in range(NEAR)]
    exists = [
        True,
        True,
        (places[2][0] >= 0) & (places[2][0] < rows),
        my_col > 0,
        my_col < cols - 1,
    ]
    first_slots = [
        0,
        jnp.where(even, 16, 12),
        jnp.where(even, 12, 16),
        4,
        8,
    ]

    def band(row_units, col_step):
        if row_units == 0:
            return 6 + col_step
        ahead, behind = {1: (10, 2), -1: (2, 10), 2: (12, 0), -2: (0, 12)}[row_units]
        return jnp.where(even, ahead, behind) + col_step

    def band_of(q, m):
        turn = -1 if q in (1, 2) else 1
        return band(ROW_STEPS[q] + turn * ROW_STEPS[m], COL_STEPS[q] + COL_STEPS[m])

    def lanes_of(o):
        if isinstance(o, int):
            return slice(o * LANES, (o + 1) * LANES)
        return pl.ds(pl.multiple_of(o * LANES, LANES), LANES)

    def when_there(q):
        def run(f):
            if exists[q] is True:
                f()
            else:
                pl.when(exists[q])(f)

        return run

    left_far = lax.rem(my_col, X_CHIPS) == 0

    barrier = pltpu.get_barrier_semaphore()
    near_count = jnp.int32(1)
    for q in range(1, NEAR):
        if q > 1:
            near_count = near_count + jnp.where(exists[q], 1, 0)

        @when_there(q)
        def _():
            pl.semaphore_signal(barrier, inc=1, device_id=places[q], device_id_type=MESH)

    for i in range(CHUNKS):
        pltpu.make_async_copy(tiles.at[:, pl.ds(i * LANES, LANES)], tp.at[:, i, :], tsem).start()
    small = [
        pltpu.make_async_copy(columns_in, columns, ssem.at[0]),
        pltpu.make_async_copy(counts_in, counts, ssem.at[1]),
        pltpu.make_async_copy(aggs_in, aggs, ssem.at[2]),
    ]
    for copy in small:
        copy.start()
    for first, last, sem in ((0, ROW_SLOTS, xsem.at[0]), (ROW_SLOTS, SLOTS, xsem.at[1])):
        for i in range(CHUNKS):
            pltpu.make_async_copy(
                stiff.at[first:last, :, pl.ds(i * LANES, LANES)], xbuf.at[first:last, :, i, :], sem
            ).start()

    lane = lax.broadcasted_iota(jnp.int32, (1, LANES), 1)
    low_half = lane < FINE

    for copy in small:
        copy.wait()
    own_groups = None
    for q in range(NEAR):
        near_row = jnp.clip(places[q][0], 0, rows - 1)
        near_col = jnp.clip(places[q][1], 0, cols - 1)
        first = (near_row * cols + near_col) * BLOCKS
        groups = [aggs[first + j] & 1 for j in range(BLOCKS)]
        word = jnp.int32(0)
        ones = jnp.int32(0)
        for j in range(BLOCKS):
            at = jnp.where(groups[j] == 1, 4 + ones, j - ones)
            word = word | (jnp.int32(j) << (4 * at))
            ones = ones + groups[j]
        if q == 0:
            own_groups = groups
        for n in range(BLOCKS):
            order[q, n] = (word >> (4 * n)) & 7

    pltpu.make_async_copy(tp, tp, tsem).wait()
    for group in range(2):
        for pair in range(2):
            a = tp[order[0, 4 * group + 2 * pair]]
            b = tp[order[0, 4 * group + 2 * pair + 1]]
            tpack[0, group, pair, pl.ds(0, CHUNKS, 2), :] = jnp.where(low_half, a, pltpu.roll(b, FINE, 1))
            tpack[0, group, pair, pl.ds(1, CHUNKS, 2), :] = jnp.where(low_half, pltpu.roll(a, FINE, 1), b)

    def tile_sem(q, group):
        return 2 * (q - 2) + group if q > 2 else q - 1

    def tile_copy(q, group):
        return pltpu.make_async_remote_copy(
            src_ref=tpack.at[0, group],
            dst_ref=tpack.at[OPPOSITE[q], group],
            send_sem=tsend.at[q - 1],
            recv_sem=trecv.at[tile_sem(OPPOSITE[q], group)],
            device_id=places[q],
            device_id_type=MESH,
        )

    def arrival(q, group):
        return pltpu.make_async_remote_copy(
            src_ref=tpack.at[0, group] if q > 2 else tpack.at[0],
            dst_ref=tpack.at[q, group] if q > 2 else tpack.at[q],
            send_sem=tsend.at[q - 1],
            recv_sem=trecv.at[tile_sem(q, group)],
            device_id=places[q],
            device_id_type=MESH,
        )

    row_at = lax.broadcasted_iota(jnp.int32, (CHUNKS, LANES), 0)
    lane_at = lax.broadcasted_iota(jnp.int32, (CHUNKS, LANES), 1)

    zero = jnp.zeros((CHUNKS, LANES), BF16)
    for q in range(NEAR):
        compact[q, 0, 0] = zero
        compact[q, 1, 0] = zero

    def spread(q, k):
        slots = first_slots[q]
        rows_k = pl.ds(pl.multiple_of(k * CHUNKS, CHUNKS), CHUNKS)
        rows_low = pl.ds(pl.multiple_of(k * CHUNKS + 256, CHUNKS), CHUNKS)
        count = counts[k, slots // ROW_SLOTS]
        word = jnp.int32(0)
        for t in range(ROW_SLOTS):
            high, low = split(xbuf[slots + t, k])
            compact[q, 0, t + 1] = high
            compact[q, 1, t + 1] = low
            word = word | jnp.where(t < count, (t + 1) << (columns[k, slots + t] * 4), 0)
        for group in range(2):
            for n in range(4):
                e = (word >> (4 * order[q, 4 * group + n])) & 7
                lanes_n = slice(n * LANES, (n + 1) * LANES)
                dense[q, group, rows_k, lanes_n] = compact[q, 0, e]
                dense[q, group, rows_low, lanes_n] = compact[q, 1, e]

    def spread_own(k, _):
        x0 = xbuf[0, k]
        diagonal = [
            jnp.sum(
                jnp.where(lane_at == 2 * row_at + p * (FINE + 1), x0, 0.0), axis=1, keepdims=True
            )
            for p in range(2)
        ]
        rows_k = pl.ds(pl.multiple_of(k * CHUNKS, CHUNKS), CHUNKS)
        damp[rows_k, :] = OMEGA / jnp.where(low_half, diagonal[0], diagonal[1])
        spread(0, k)
        return 0

    def spread_near(k, _):
        for q in range(1, NEAR):
            spread(q, k)
        return 0

    def smooth_half(q, group):
        for pair in range(2):
            v = tpack[q, group, pair]
            r = pltpu.roll(v, FINE, 1)
            for part, (v_part, r_part) in enumerate(zip(split(v), split(r))):
                lanes_part = slice(part * LANES, (part + 1) * LANES)
                none = jnp.zeros_like(v_part)
                tiles_at = (
                    jnp.where(low_half, v_part, none),
                    jnp.where(low_half, none, r_part),
                    jnp.where(low_half, r_part, none),
                    jnp.where(low_half, none, v_part),
                )
                for n in range(4):
                    rows_n = slice((4 * pair + n) * FINE, (4 * pair + n + 1) * FINE)
                    weights[q, group, rows_n, lanes_part] = tiles_at[n]
        x = dot(dense[q, group, :256], weights[q, group])
        y = dot(dense[q, group, 256:], weights[q, group, :, :LANES])
        s = x[:, :LANES] + (x[:, LANES:] + y)
        halves[q, group] = s
        l = -(damp[...] * s)
        if q == 0:
            own = [jnp.where(own_groups[k] == group, tp[k], 0.0) for k in range(BLOCKS)]
            l = l + jnp.concatenate(own, axis=0)
        first = q * LANES + group * FINE
        for part, l_part in enumerate(split(l.T)):
            for p in range(2):
                left[part, first : first + FINE, p * 256 : (p + 1) * 256] = l_part[p * FINE : (p + 1) * FINE]

    def make_right(q):
        s_0, s_1 = halves[q, 0], halves[q, 1]
        by_parity = (
            jnp.where(low_half, s_0, pltpu.roll(s_1, FINE, 1)),
            jnp.where(low_half, pltpu.roll(s_0, FINE, 1), s_1),
        )
        for p in range(2):
            for part, r_part in enumerate(split(by_parity[p])):
                right[part, p * 256 : (p + 1) * 256, lanes_of(q)] = r_part

    def smooth(q):
        smooth_half(q, 0)
        smooth_half(q, 1)
        make_right(q)

    def products(row_list, m_from, m_to):
        cols_r = slice(m_from * LANES, m_to * LANES)
        highs = jnp.concatenate([left[0, a : a + n, :] for a, n in row_list], axis=0)
        lows = jnp.concatenate([left[1, a : a + n, :] for a, n in row_list], axis=0)
        return (
            dot(highs, right[0, :, cols_r])
            + dot(lows, right[0, :, cols_r])
            + dot(highs, right[1, :, cols_r])
        )

    square_row = lax.broadcasted_iota(jnp.int32, (FINE, FINE), 0)
    square_col = lax.broadcasted_iota(jnp.int32, (FINE, FINE), 1)

    def packed(g):
        a, b, c = g[:FINE, :FINE], g[:FINE, FINE:], g[FINE:, FINE:]
        square = jnp.where(square_row >= square_col, a, c)
        diagonal = jnp.sum(jnp.where(square_row == square_col, c, 0.0), axis=0, keepdims=True)
        top = jnp.concatenate([square, b], axis=1)
        last = jnp.broadcast_to(jnp.concatenate([diagonal, diagonal], axis=1), (8, LANES))
        return jnp.concatenate([top, last], axis=0)

    def unpacked(x):
        square, b = x[:FINE, :FINE], x[:FINE, FINE:]
        diagonal = x[FINE : FINE + 1, :FINE]
        turned = x[:FINE].T
        square_t, b_t = turned[:FINE], turned[FINE:]
        a = jnp.where(square_row >= square_col, square, square_t)
        c = jnp.where(square_row < square_col, square, square_t)
        c = jnp.where(square_row == square_col, diagonal, c)
        return jnp.concatenate(
            [jnp.concatenate([a, b], axis=1), jnp.concatenate([b_t, c], axis=1)], axis=0
        )

    def set_sem(q, m):
        return 0 if q == 1 else 1 + 4 * (q - 2) + max(m - 1, 0)

    def piece_copy(q, m, group):
        to = OPPOSITE[q]
        recv_sem = grecv_sem.at[set_sem(to, m)]
        if m == q and q > 1:
            return pltpu.make_async_remote_copy(
                src_ref=psend.at[q - 1],
                dst_ref=precv.at[to - 1],
                send_sem=psend_sem.at[q - 1],
                recv_sem=recv_sem,
                device_id=places[q],
                device_id_type=MESH,
            )
        at = pl.ds(0, LANES) if group is None else pl.ds(group * FINE, FINE)
        return pltpu.make_async_remote_copy(
            src_ref=gsend.at[q, m, at],
            dst_ref=grecv.at[to, m, at],
            send_sem=gsend_sem.at[q - 1],
            recv_sem=recv_sem,
            device_id=places[q],
            device_id_type=MESH,
        )

    def set_arrival(q, m_from, m_to):
        alone = m_from == OPPOSITE[q] and q > 1
        return pltpu.make_async_remote_copy(
            src_ref=psend.at[q - 1] if alone else gsend.at[q, m_from:m_to],
            dst_ref=precv.at[q - 1] if alone else grecv.at[q, m_from:m_to],
            send_sem=gsend_sem.at[q - 1],
            recv_sem=grecv_sem.at[set_sem(q, m_from)],
            device_id=places[q],
            device_id_type=MESH,
        )

    def all_sent(q):
        pltpu.make_async_remote_copy(
            src_ref=tpack.at[0],
            dst_ref=tpack.at[OPPOSITE[q]],
            send_sem=tsend.at[q - 1],
            recv_sem=trecv.at[tile_sem(q, 0)],
            device_id=places[q],
            device_id_type=MESH,
        ).wait_send()
        pltpu.make_async_remote_copy(
            src_ref=gsend.at[q, 0:4] if q > 1 else gsend.at[q],
            dst_ref=grecv.at[q, 0:4] if q > 1 else grecv.at[q],
            send_sem=gsend_sem.at[q - 1],
            recv_sem=grecv_sem.at[set_sem(q, 0)],
            device_id=places[q],
            device_id_type=MESH,
        ).wait_send()
        if q > 1:
            piece_copy(q, q, None).wait_send()

    def start_pieces(q, m_from, m_to, group):
        @when_there(q)
        def _():
            for m in sorted(range(m_from, m_to), key=lambda m: m != q):
                piece_copy(q, m, group).start()

    def make_and_send(q_list, m_from, m_to):
        g = products([(q * LANES, LANES) for q in q_list], m_from, m_to)
        for at, q in enumerate(q_list):
            for m in range(m_from, m_to):
                part = g[at * LANES : (at + 1) * LANES, (m - m_from) * LANES : (m - m_from + 1) * LANES]
                if q == 0:
                    out[:, lanes_of(band_of(0, m))] = part
                elif m == q and q > 1:
                    psend[q - 1] = packed(part)
                else:
                    gsend[q, m] = part
        if q_list == (3, 4):
            far_first(lambda q: start_pieces(q, m_from, m_to, None))
        else:
            for q in q_list:
                if q > 0:
                    start_pieces(q, m_from, m_to, None)

    def make_and_send_halves(group, m_from, m_to):
        g = products([(q * LANES + group * FINE, FINE) for q in (3, 4)], m_from, m_to)
        for at, q in enumerate((3, 4)):
            for m in range(m_from, m_to):
                gsend[q, m, group * FINE : (group + 1) * FINE] = g[
                    at * FINE : (at + 1) * FINE, (m - m_from) * LANES : (m - m_from + 1) * LANES
                ]
        far_first(lambda q: start_pieces(q, m_from, m_to, group))

    def wait_tiles(q, group):
        @when_there(q)
        def _():
            arrival(q, group).wait_recv()

    pl.semaphore_wait(barrier, near_count)
    def send_tiles(q, group):
        @when_there(q)
        def _():
            tile_copy(q, group).start()

    def far_first(send):
        @pl.when(left_far)
        def _():
            send(3)
            send(4)

        @pl.when(jnp.logical_not(left_far))
        def _():
            send(4)
            send(3)

    for group in range(2):
        far_first(lambda q: send_tiles(q, group))
        for q in (2, 1):
            send_tiles(q, group)

    for q in range(2, NEAR):

        @pl.when(jnp.logical_not(exists[q]))
        def _():
            tpack[q] = jnp.zeros((2, 2, FINE, LANES), F32)

    for o in range(OFFSETS):
        if o not in (2, 5, 6, 7, 10):
            out[:, lanes_of(o)] = jnp.zeros((LANES, LANES), F32)

    pltpu.make_async_copy(xbuf.at[0:ROW_SLOTS], xbuf.at[0:ROW_SLOTS], xsem.at[0]).wait()
    lax.fori_loop(0, BLOCKS, spread_own, 0)
    pltpu.make_async_copy(xbuf.at[ROW_SLOTS:SLOTS], xbuf.at[ROW_SLOTS:SLOTS], xsem.at[1]).wait()
    lax.fori_loop(0, BLOCKS, spread_near, 0)
    smooth(0)
    wait_tiles(1, 0)
    smooth(1)
    make_and_send((0, 1), 0, 2)
    for group in range(2):
        wait_tiles(3, group)
        wait_tiles(4, group)
        smooth_half(3, group)
        smooth_half(4, group)
        make_and_send_halves(group, 0, 2)
    wait_tiles(2, 0)
    smooth(2)
    make_and_send((2,), 0, 2)
    make_right(3)
    make_right(4)
    make_and_send((3, 4), 3, 5)
    make_and_send((2,), 2, 5)
    make_and_send((3, 4), 2, 3)
    make_and_send((0, 1), 2, 5)

    for q_list, m_from, m_to in (
        ((3, 4), 0, 2),
        ((2,), 0, 2),
        ((1,), 0, 5),
        ((2,), 2, 3),
        ((2,), 3, 4),
        ((2,), 4, 5),
        ((4,), 3, 4),
        ((3,), 4, 5),
        ((3,), 3, 4),
        ((4,), 4, 5),
        ((3, 4), 2, 3),
    ):
        for q in q_list:

            @when_there(q)
            def _():
                set_arrival(q, m_from, m_to).wait_recv()
                for m in range(m_from, m_to):
                    o = lanes_of(band_of(q, m))
                    if q > 1 and m == OPPOSITE[q]:
                        out[:, o] += unpacked(precv[q - 1])
                    else:
                        out[:, o] += grecv[q, m]

    for q in range(1, NEAR):

        @when_there(q)
        def _():
            all_sent(q)


def solution(mesh):
    rows, cols = mesh.shape["row"], mesh.shape["col"]

    def body(stiffness_blocks, block_columns, block_counts, tentative_tiles, aggregate_of):
        any_spec = pl.BlockSpec(memory_space=pl.ANY)
        in_hbm = lambda x: pltpu.with_memory_space_constraint(x, pltpu.HBM)
        dma = pltpu.SemaphoreType.DMA
        result = pl.pallas_call(
            lambda *refs: kernel(rows, cols, *refs),
            out_shape=jax.ShapeDtypeStruct((2 * FINE, OFFSETS * LANES), F32),
            in_specs=[any_spec] * 5,
            out_specs=pl.BlockSpec(memory_space=pltpu.VMEM),
            scratch_shapes=[
                pltpu.SMEM((BLOCKS, SLOTS), jnp.int32),
                pltpu.SMEM((BLOCKS, NEAR), jnp.int32),
                pltpu.SMEM(aggregate_of.shape, jnp.int32),
                pltpu.VMEM((SLOTS, BLOCKS, CHUNKS, LANES), F32),
                pltpu.VMEM((NEAR, 2, 8, CHUNKS, LANES), BF16),
                pltpu.VMEM((NEAR, 2, 2 * BLOCKS * CHUNKS, 4 * LANES), BF16),
                pltpu.SMEM((NEAR, BLOCKS), jnp.int32),
                pltpu.VMEM((BLOCKS, CHUNKS, LANES), F32),
                pltpu.VMEM((NEAR, 2, 2, FINE, LANES), F32),
                pltpu.VMEM((NEAR, 2, 4 * LANES, 2 * LANES), BF16),
                pltpu.VMEM((NEAR, 2, BLOCKS * CHUNKS, LANES), F32),
                pltpu.VMEM((BLOCKS * CHUNKS, LANES), F32),
                pltpu.VMEM((2, BLOCKS * FINE, NEAR * LANES), BF16),
                pltpu.VMEM((2, NEAR * LANES, BLOCKS * FINE), BF16),
                pltpu.VMEM((NEAR, NEAR, LANES, LANES), F32),
                pltpu.VMEM((NEAR, NEAR, LANES, LANES), F32),
                pltpu.VMEM((NEAR - 1, FINE + 8, LANES), F32),
                pltpu.VMEM((NEAR - 1, FINE + 8, LANES), F32),
                dma((2,)),
                dma,
                dma((3,)),
                dma((NEAR - 1,)),
                dma((6,)),
                dma((NEAR - 1,)),
                dma((NEAR - 1,)),
                dma((13,)),
            ],
            compiler_params=pltpu.CompilerParams(
                collective_id=0, has_side_effects=True, vmem_limit_bytes=40 << 20
            ),
        )(
            in_hbm(jnp.transpose(stiffness_blocks, (1, 0, 2))),
            in_hbm(block_columns),
            in_hbm(block_counts),
            in_hbm(tentative_tiles),
            in_hbm(aggregate_of),
        )
        return result.reshape(2, FINE, OFFSETS * LANES)

    by_device = P(("row", "col"), None)
    by_device3 = P(("row", "col"), None, None)
    return jax.shard_map(
        body,
        mesh=mesh,
        in_specs=(by_device3, by_device, by_device, by_device, P()),
        out_specs=by_device3,
        check_vma=False,
    )
```
